32 devices in a mesh: dp: 16 (over z, x, core), seq: 2 (over y).
Axes of the slice: x: 2, y: 2, z: 4, core: 2. Of those that a mesh axis runs over, the one named last changes fastest.
Arguments:
- inputs: float32 [16, 512, 1280], P('dp', 'seq'), may hold values from -6 to 6
- cotangent: float32 [16, 512, 1280], P('dp', 'seq'), may hold values from -6 to 6
- starts: int32 [16, 4], P('dp'), may hold values from 0 to 511, as said below
- weights: float32 [1280, 7680], P('dp')
- weight_m: float32 [1280, 7680], P('dp')
- weight_v: float32 [1280, 7680], P('dp')
- gains: float32 [2, 1280], P(None, 'dp'), may hold values from 0.5 to 1.5
- gain_m: float32 [2, 1280], P(None, 'dp'), may hold values from -512 to 512
- gain_v: float32 [2, 1280], P(None, 'dp'), may hold values from 8192 to 32768
- qscale: float32 [80], replicated, may hold values from -3 to 3
- qscale_m: float32 [80], replicated, may hold values from -512 to 512
- qscale_v: float32 [80], replicated, may hold values from 8192 to 32768
Outputs:
- outputs: float32 [16, 512, 1280], P('dp', 'seq')
- input_grad: float32 [16, 512, 1280], P('dp', 'seq')
- weights_new: float32 [1280, 7680], P('dp')
- weight_m_new: float32 [1280, 7680], P('dp')
- weight_v_new: float32 [1280, 7680], P('dp')
- weights_low: bfloat16 [1280, 7680], P('dp')
- gains_new: float32 [2, 1280], P(None, 'dp')
- gain_m_new: float32 [2, 1280], P(None, 'dp')
- gain_v_new: float32 [2, 1280], P(None, 'dp')
- qscale_new: float32 [80], replicated
- qscale_m_new: float32 [80], replicated
- qscale_v_new: float32 [80], replicated
The draws below stay inside these ranges and needn't reach their ends.
Inputs may be any that keep to these rules, and one draw needn't show every extreme that they name: `starts`: each row is 4 increasing start positions, the first 0; one document of each stream begins within the first 256 positions and ends within the last 256.
All inputs are finite; a program needn't handle non-finite values.
Results may differ from the reference program's by a relative error of at most 0.022.
The reference program's roundings to bfloat16 on the way count: a program that leaves them out, or rounds other values in their place, can miss the bound.
Values may be sent and summed in bfloat16 or wider, within the bound.
A program may use at most 192 MiB of HBM per device.

```python
import math
import jax
import jax.numpy as jnp
from jax import lax

D = 1280
HEADS = 16
HD = 80
TOK_DEV = 256
STEP = 10
STREAMS = 16
LEN = 512


def column_factor(factors):
    column = jnp.arange(6 * D, dtype=jnp.int32) // D
    table = jnp.array(factors, dtype=jnp.float32)
    picks = column[:, None] == jnp.arange(6, dtype=jnp.int32)[None, :]
    return jnp.sum(jnp.where(picks, table[None, :], 0.0), axis=1)


def grad_factor():
    return column_factor([2.0, 2.0, 1.0, 0.1, 0.5, 0.4]) * jnp.sqrt(jnp.float32(STREAMS * LEN))


def draw_starts(key, part):
    key = jax.random.fold_in(key, 11)
    key_a, key_b, key_c = jax.random.split(key, 3)
    first = jax.random.randint(key_a, (STREAMS,), 1, TOK_DEV, dtype=jnp.int32)
    third = LEN - TOK_DEV + 1 + jax.random.randint(key_b, (STREAMS,), 0, TOK_DEV // 2, dtype=jnp.int32)
    room = LEN - third - 1
    fourth = third + 1 + jax.random.randint(key_c, (STREAMS,), 0, room, dtype=jnp.int32)
    zeros = jnp.zeros((STREAMS,), jnp.int32)
    return jnp.stack([zeros, first, third, fourth], axis=1)


def draw_weights(key, part):
    key = jax.random.fold_in(key, 21)
    factor = column_factor([1.0, 1.0, 1.0, 4.0, 1.0, 1.0]) / jnp.sqrt(jnp.float32(D))
    return jax.random.normal(key, (D, 6 * D), jnp.float32) * factor[None, :]


def draw_weight_m(key, part):
    key = jax.random.fold_in(key, 31)
    return jax.random.normal(key, (D, 6 * D), jnp.float32) * grad_factor()[None, :]


def draw_weight_v(key, part):
    key = jax.random.fold_in(key, 41)
    spread = jnp.exp(jax.random.uniform(key, (D, 6 * D), jnp.float32, 0.0, jnp.log(4.0)))
    scale = grad_factor()
    return spread * (scale * scale)[None, :]


def levels(own_key, extent, pieces, least, largest):
    level = 1.0
    for dim, blocks in pieces:
        steps = jax.random.uniform(jax.random.fold_in(jax.random.fold_in(own_key, 6), dim), (blocks,), jnp.float32, least / len(pieces), largest / len(pieces))
        level = level * jnp.repeat(jnp.exp(steps), extent[dim] // blocks).reshape((-1,) + (1,) * (len(extent) - 1 - dim))
    return level


def gaussian(own_key, dims, deviation, bound, pieces=(), kind=jnp.bfloat16):
    entries = deviation * jax.random.normal(own_key, dims, jnp.float32)
    if pieces:
        entries = entries * levels(own_key, dims, pieces, -0.22, 0.18)
    return jnp.clip(entries, -bound, bound).astype(kind)


def setup_inputs(seed: int = 0) -> dict:
    streams_of = jax.random.split(jax.random.key(seed), 13)
    inputs = gaussian(streams_of[0], (STREAMS, LEN, D), 1.0, 6.0, ((0, 16), (1, 2)), jnp.float32)
    cotangent = gaussian(streams_of[1], (STREAMS, LEN, D), 1.0, 6.0, ((0, 16), (1, 2)), jnp.float32)
    starts = draw_starts(jax.random.fold_in(streams_of[12], 71), 0)
    weights = draw_weights(jax.random.fold_in(streams_of[12], 71), 0)
    weight_m = draw_weight_m(jax.random.fold_in(streams_of[12], 71), 0)
    weight_v = draw_weight_v(jax.random.fold_in(streams_of[12], 71), 0)
    gains = jnp.clip(1.0 + 0.1 * jax.random.normal(streams_of[6], (2, D), jnp.float32), 0.5, 1.5)
    gain_m = gaussian(streams_of[7], (2, D), ((STREAMS * LEN) ** 0.5), 512.0, ((1, 16),), jnp.float32)
    gain_v = jnp.clip(jnp.exp(math.log(32768.0) - 1.3862944 * jax.random.uniform(streams_of[8], (2, D), jnp.float32) ** levels(streams_of[8], (2, D), ((1, 16),), -0.2, 0.2)), 8192.0, 32768.0)
    qscale = gaussian(streams_of[9], (HD,), 1.0, 3.0, (), jnp.float32)
    qscale_m = gaussian(streams_of[10], (HD,), ((STREAMS * LEN) ** 0.5), 512.0, (), jnp.float32)
    qscale_v = jnp.clip(jnp.exp(jax.random.uniform(streams_of[11], (HD,), jnp.float32, math.log(8192.0), math.log(32768.0))), 8192.0, 32768.0)
    return dict(inputs=inputs, cotangent=cotangent, starts=starts, weights=weights, weight_m=weight_m, weight_v=weight_v, gains=gains, gain_m=gain_m, gain_v=gain_v, qscale=qscale, qscale_m=qscale_m, qscale_v=qscale_v)


EPS = 1e-06
QUERY_BASE = 1.442695
BETA_ONE = 0.5
BETA_TWO = 0.5
ADAM_EPS = 1e-08
RATE_MATRIX = 0.02
RATE_GAIN = 0.3
DECAY = 0.1
NEG = -1e+30

@jax.custom_vjp
def low(v):
    return lax.optimization_barrier(v.astype(jnp.bfloat16)).astype(jnp.float32)

@jax.custom_vjp
def low_back(v):
    return v

def low_keep(v):
    return (low(v), None)

def low_pass(kept, grad):
    return (grad,)

def back_keep(v):
    return (v, None)

def back_low(kept, grad):
    return (low(grad),)
low.defvjp(low_keep, low_pass)
low_back.defvjp(back_keep, back_low)

def matmul(left, right):
    return jnp.dot(left, right, precision=lax.Precision.HIGHEST, preferred_element_type=jnp.float32)

def rms_norm(values, gain):
    inverse = lax.rsqrt(lax.optimization_barrier(jnp.mean(values * values, axis=-1, keepdims=True)) + EPS)
    return values * inverse * gain

def attend(queries, keys, values, segment):
    block = min(512, LEN)
    positions = jnp.arange(LEN, dtype=jnp.int32)

    def one_block(index):
        start = (index * block).astype(jnp.int32)
        query_block = lax.dynamic_slice_in_dim(queries, start, block, 0)
        raw = low_back(jnp.einsum('qhd,khd->hqk', query_block, keys, precision=lax.Precision.HIGHEST))
        rows = start + jnp.arange(block, dtype=jnp.int32)
        row_seg = lax.dynamic_slice_in_dim(segment, start, block, 0)
        allowed = (positions[None, :] <= rows[:, None]) & (segment[None, :] == row_seg[:, None])
        masked = jnp.where(allowed[None], raw, NEG)
        top = lax.optimization_barrier(jnp.max(masked, axis=-1, keepdims=True))
        expo = jnp.exp(masked - top)
        probs = low(expo / lax.optimization_barrier(jnp.sum(expo, axis=-1, keepdims=True)))
        return jnp.einsum('hqk,khd->qhd', probs, values, precision=lax.Precision.HIGHEST)
    outs = lax.map(jax.checkpoint(one_block), jnp.arange(LEN // block, dtype=jnp.int32))
    return outs.reshape(LEN, HEADS * HD)

def layer(resid, weights, gains, qscale, segment):
    low_w = low(weights)
    low_g = low(gains)
    w_qkv = low_w[:, :3 * D]
    w_out = low_w[:, 3 * D:4 * D]
    w_up = low_w[:, 4 * D:5 * D]
    w_down = low_w[:, 5 * D:]
    hidden_one = low(rms_norm(resid, low_g[0]))
    projected = matmul(hidden_one, w_qkv)
    query = low_back(projected[:, :D])
    key_part = projected[:, D:2 * D]
    value_part = projected[:, 2 * D:]
    scale = QUERY_BASE / math.sqrt(HD) * jax.nn.softplus(qscale)
    scaled = query * jnp.tile(scale, HEADS)
    q_low = low_back(low(scaled)).reshape(LEN, HEADS, HD)
    k_low = low_back(low(key_part)).reshape(LEN, HEADS, HD)
    v_low = low_back(low(value_part)).reshape(LEN, HEADS, HD)
    attended = low_back(low(attend(q_low, k_low, v_low, segment)))
    mixed = resid + low_back(matmul(attended, w_out))
    hidden_two = low(rms_norm(mixed, low_g[1]))
    gate = low_back(matmul(hidden_two, w_up))
    activ = low(jax.nn.silu(gate))
    return mixed + low_back(matmul(activ, w_down))

def adamw(param, grad, first, second, rate):
    first_new = BETA_ONE * first + (1.0 - BETA_ONE) * grad
    second_new = BETA_TWO * second + (1.0 - BETA_TWO) * grad * grad
    first_hat = first_new / (1.0 - BETA_ONE ** STEP)
    second_hat = second_new / (1.0 - BETA_TWO ** STEP)
    param_new = param - rate * (first_hat / (jnp.sqrt(second_hat) + ADAM_EPS) + DECAY * param)
    return (param_new, first_new, second_new)

def reference(inputs, cotangent, starts, weights, weight_m, weight_v, gains, gain_m, gain_v, qscale, qscale_m, qscale_v):
    positions = jnp.arange(LEN, dtype=jnp.int32)

    def one_stream(carry, item):
        resid, grad_out, stream_starts = item
        segment = lax.optimization_barrier(jnp.sum((positions[:, None] >= stream_starts[None, :]).astype(jnp.int32), axis=1)) - 1

        def forward(x_val, w_val, g_val, s_val):
            return layer(x_val, w_val, g_val, s_val, segment)
        result, pull = jax.vjp(forward, resid, weights, gains, qscale)
        d_input, d_weights, d_gains, d_scale = pull(grad_out)
        new_carry = (carry[0] + d_weights, carry[1] + d_gains, carry[2] + d_scale)
        return (new_carry, (result, d_input))
    start_carry = (jnp.zeros((D, 6 * D), jnp.float32), jnp.zeros((2, D), jnp.float32), jnp.zeros((HD,), jnp.float32))
    sums, (outputs, input_grad) = lax.scan(one_stream, start_carry, (inputs, cotangent, starts))
    weights_new, weight_m_new, weight_v_new = adamw(weights, sums[0], weight_m, weight_v, RATE_MATRIX)
    gains_new, gain_m_new, gain_v_new = adamw(gains, sums[1], gain_m, gain_v, RATE_GAIN)
    qscale_new, qscale_m_new, qscale_v_new = adamw(qscale, sums[2], qscale_m, qscale_v, RATE_GAIN)
    return (outputs, input_grad, weights_new, weight_m_new, weight_v_new, weights_new.astype(jnp.bfloat16), gains_new, gain_m_new, gain_v_new, qscale_new, qscale_m_new, qscale_v_new)
```

```python
import functools
import math
import types

import jax
import jax.numpy as jnp
from jax import lax
from jax.experimental import pallas as pl
from jax.experimental.pallas import tpu as pltpu
from jax.sharding import PartitionSpec as P

HEADS = 16
STEP = 10


EPS = 1e-06
QUERY_BASE = 1.442695
BETA_ONE = 0.5
BETA_TWO = 0.5
ADAM_EPS = 1e-08
RATE_MATRIX = 0.02
RATE_GAIN = 0.3
DECAY = 0.1
NEG = -1e30


def norm_forward(values, gain):
    inverse = lax.rsqrt(jnp.mean(values * values, axis=-1, keepdims=True) + EPS)
    normed = values * inverse
    return (normed, inverse, (normed * gain).astype(jnp.bfloat16))


def norm_backward(grad, normed, inverse, gain):
    gain_grad = jnp.sum(grad * normed, axis=0)
    scaled = grad * gain
    return (
        inverse * (scaled - normed * jnp.mean(scaled * normed, axis=-1, keepdims=True)),
        gain_grad,
    )


def adamw(param, grad, first, second, rate):
    first_new = BETA_ONE * first + (1.0 - BETA_ONE) * grad
    second_new = BETA_TWO * second + (1.0 - BETA_TWO) * grad * grad
    first_hat = first_new / (1.0 - BETA_ONE**STEP)
    second_hat = second_new / (1.0 - BETA_TWO**STEP)
    param_new = param - rate * (first_hat / (jnp.sqrt(second_hat) + ADAM_EPS) + DECAY * param)
    return (param_new, first_new, second_new)


def plain_layer(
    inputs,
    cotangent,
    starts,
    weights,
    weight_m,
    weight_v,
    gains,
    gain_m,
    gain_v,
    qscale,
    qscale_m,
    qscale_v,
):
    full_w, full_g = (
        lax.all_gather(weights.astype(jnp.bfloat16), "dp", axis=0, tiled=True),
        lax.all_gather(gains.astype(jnp.bfloat16), "dp", axis=1, tiled=True),
    )
    width = full_w.shape[0]
    head_dim = width // HEADS
    w_qkv = full_w[:, : 3 * width]
    w_out = full_w[:, 3 * width : 4 * width]
    w_up = full_w[:, 4 * width : 5 * width]
    w_down = full_w[:, 5 * width :]
    gain_one = full_g[0].astype(jnp.float32)
    gain_two = full_g[1].astype(jnp.float32)
    resid = inputs[0]
    count = resid.shape[0]
    groups = lax.axis_size("seq")
    length = count * groups
    local_width = width // groups
    local_heads = local_width // head_dim
    block = min(512, length)
    blocks = length // block
    normed_one, inverse_one, hidden_one = norm_forward(resid, gain_one)
    projected = jnp.dot(hidden_one, w_qkv, preferred_element_type=jnp.float32).reshape(
        count, 3, width
    )
    base_scale = QUERY_BASE / math.sqrt(head_dim)
    tiled = jnp.tile(base_scale * jax.nn.softplus(qscale), HEADS)
    factor = jnp.stack([tiled, jnp.ones_like(tiled), jnp.ones_like(tiled)])
    outgoing = (projected * factor[None]).astype(jnp.bfloat16)
    arrived = lax.all_to_all(outgoing, "seq", split_axis=2, concat_axis=0, tiled=True)
    queries = arrived[:, 0].reshape(length, local_heads, head_dim)
    keys = arrived[:, 1].reshape(length, local_heads, head_dim)
    values = arrived[:, 2].reshape(length, local_heads, head_dim)
    positions = jnp.arange(length, dtype=jnp.int32)
    segment = jnp.sum((positions[:, None] >= starts[0][None, :]).astype(jnp.int32), axis=1) - 1

    def masked_scores(start):
        query_block = lax.dynamic_slice_in_dim(queries, start, block, 0)
        raw = jnp.einsum("qhd,khd->hqk", query_block, keys, preferred_element_type=jnp.float32)
        rows = start + jnp.arange(block, dtype=jnp.int32)
        row_seg = lax.dynamic_slice_in_dim(segment, start, block, 0)
        allowed = (positions[None, :] <= rows[:, None]) & (segment[None, :] == row_seg[:, None])
        return (query_block, jnp.where(allowed[None], raw, NEG))

    def forward_block(index):
        query_block, masked = masked_scores(index * block)
        top = jnp.max(masked, axis=-1, keepdims=True)
        expo = jnp.exp(masked - top)
        total = jnp.sum(expo, axis=-1, keepdims=True)
        probs = (expo / total).astype(jnp.bfloat16)
        attended = jnp.einsum("hqk,khd->qhd", probs, values, preferred_element_type=jnp.float32)
        return (attended.astype(jnp.bfloat16), (top + jnp.log(total))[..., 0])

    head_out, log_totals = lax.map(forward_block, jnp.arange(blocks, dtype=jnp.int32))
    head_out = head_out.reshape(length, local_width)
    attn_rows = lax.all_to_all(head_out, "seq", split_axis=0, concat_axis=1, tiled=True)
    mixed = resid + jnp.dot(attn_rows, w_out, preferred_element_type=jnp.float32)
    normed_two, inverse_two, hidden_two = norm_forward(mixed, gain_two)
    gate = jnp.dot(hidden_two, w_up, preferred_element_type=jnp.float32)
    sigma = jax.nn.sigmoid(gate)
    activ = (gate * sigma).astype(jnp.bfloat16)
    outputs = mixed + jnp.dot(activ, w_down, preferred_element_type=jnp.float32)
    grad_top = cotangent[0]
    grad_low = grad_top.astype(jnp.bfloat16)
    grad_activ = jnp.dot(grad_low, w_down.T, preferred_element_type=jnp.float32)
    grad_gate = (grad_activ * sigma * (1.0 + gate * (1.0 - sigma))).astype(jnp.bfloat16)
    grad_down = jnp.dot(activ.T, grad_low, preferred_element_type=jnp.float32)
    grad_up = jnp.dot(hidden_two.T, grad_gate, preferred_element_type=jnp.float32)
    grad_hidden_two = jnp.dot(grad_gate, w_up.T, preferred_element_type=jnp.float32)
    grad_norm_two, gain_grad_two = norm_backward(grad_hidden_two, normed_two, inverse_two, gain_two)
    grad_mixed = grad_top + grad_norm_two
    mixed_low = grad_mixed.astype(jnp.bfloat16)
    grad_out = jnp.dot(attn_rows.T, mixed_low, preferred_element_type=jnp.float32)
    grad_attn = jnp.dot(mixed_low, w_out.T, preferred_element_type=jnp.float32).astype(jnp.bfloat16)
    grad_heads = lax.all_to_all(grad_attn, "seq", split_axis=1, concat_axis=0, tiled=True).reshape(
        length, local_heads, head_dim
    )

    def backward_block(carry, index):
        key_sum, value_sum = carry
        start = index * block
        query_block, masked = masked_scores(start)
        grad_block = lax.dynamic_slice_in_dim(grad_heads, start, block, 0)
        lse_block = log_totals[index]
        probs = jnp.exp(masked - lse_block[:, :, None])
        value_sum = value_sum + jnp.einsum(
            "hqk,qhd->khd",
            probs.astype(jnp.bfloat16),
            grad_block,
            preferred_element_type=jnp.float32,
        )
        grad_probs = jnp.einsum(
            "qhd,khd->hqk", grad_block, values, preferred_element_type=jnp.float32
        )
        grad_scores = probs * (grad_probs - jnp.sum(probs * grad_probs, axis=-1, keepdims=True))
        scores_low = grad_scores.astype(jnp.bfloat16)
        grad_query = jnp.einsum(
            "hqk,khd->qhd", scores_low, keys, preferred_element_type=jnp.float32
        )
        key_sum = key_sum + jnp.einsum(
            "hqk,qhd->khd", scores_low, query_block, preferred_element_type=jnp.float32
        )
        return ((key_sum, value_sum), grad_query)

    empty = jnp.zeros((length, local_heads, head_dim), jnp.float32)
    (key_grad, value_grad), query_grad = lax.scan(
        backward_block, (empty, empty), jnp.arange(blocks, dtype=jnp.int32)
    )
    stacked = jnp.stack(
        [
            query_grad.reshape(length, local_width),
            key_grad.reshape(length, local_width),
            value_grad.reshape(length, local_width),
        ],
        axis=1,
    ).astype(jnp.bfloat16)
    returned = lax.all_to_all(stacked, "seq", split_axis=0, concat_axis=2, tiled=True)
    scaled_grad = returned[:, 0].astype(jnp.float32)
    scale_part = jnp.sum(scaled_grad * projected[:, 0], axis=0).reshape(HEADS, head_dim).sum(axis=0)
    query_low = (scaled_grad * tiled[None]).astype(jnp.bfloat16)
    grad_qkv_rows = jnp.concatenate([query_low[:, None], returned[:, 1:]], axis=1).reshape(
        count, 3 * width
    )
    grad_qkv = jnp.dot(hidden_one.T, grad_qkv_rows, preferred_element_type=jnp.float32)
    grad_hidden_one = jnp.dot(grad_qkv_rows, w_qkv.T, preferred_element_type=jnp.float32)
    grad_norm_one, gain_grad_one = norm_backward(grad_hidden_one, normed_one, inverse_one, gain_one)
    input_grad = grad_mixed + grad_norm_one
    all_grads = jnp.concatenate([grad_qkv, grad_out, grad_up, grad_down], axis=1)
    gain_grads = jnp.stack([gain_grad_one, gain_grad_two])
    owned_w, owned_g = (
        lax.psum_scatter(
            all_grads.astype(jnp.bfloat16), "dp", scatter_dimension=0, tiled=True
        ).astype(jnp.float32),
        lax.psum_scatter(
            gain_grads.astype(jnp.bfloat16), "dp", scatter_dimension=1, tiled=True
        ).astype(jnp.float32),
    )
    owned_w, owned_g = (
        lax.psum(owned_w.astype(jnp.bfloat16), "seq").astype(jnp.float32),
        lax.psum(owned_g.astype(jnp.bfloat16), "seq").astype(jnp.float32),
    )
    scale_grad = lax.psum(scale_part, ("dp", "seq")) * base_scale * jax.nn.sigmoid(qscale)
    weights_new, weight_m_new, weight_v_new = adamw(
        weights, owned_w, weight_m, weight_v, RATE_MATRIX
    )
    gains_new, gain_m_new, gain_v_new = adamw(gains, owned_g, gain_m, gain_v, RATE_GAIN)
    qscale_new, qscale_m_new, qscale_v_new = adamw(
        qscale, scale_grad, qscale_m, qscale_v, RATE_GAIN
    )
    return (
        outputs[None],
        input_grad[None],
        weights_new,
        weight_m_new,
        weight_v_new,
        weights_new.astype(jnp.bfloat16),
        gains_new,
        gain_m_new,
        gain_v_new,
        qscale_new,
        qscale_m_new,
        qscale_v_new,
    )


MESH = pl.DeviceIdType.MESH
BF = jnp.bfloat16
F32 = jnp.float32
DEPTH = 4
STEP_ROWS = 32
UNITS = 8
TREE = ("o", "O", "d", "D")
VMEM_BYTES = 64 * 1024 * 1024


class Hop:
    def __init__(self, number, sems, source, target, arriving, device, when=None, into=None):
        self.number, self.when, self.pending = number, when, True
        self.out = self.describe(number, into or number, sems, source, target, device)
        if arriving is not None:
            self.back = self.describe(number, number, sems, arriving, arriving, device)
        self.guard(self.out.start)

    @staticmethod
    def describe(number, into, sems, source, target, device):
        return pltpu.make_async_remote_copy(
            src_ref=source,
            dst_ref=target,
            send_sem=sems[0].at[number],
            recv_sem=sems[1].at[into],
            device_id=device,
            device_id_type=MESH,
        )

    def guard(self, action):
        if self.when is None:
            action()
        else:
            pl.when(self.when)(action)

    def arrived(self):
        self.back.wait_recv()

    def left(self):
        if self.pending:
            self.guard(self.out.wait_send)
        self.pending = False


def dot_nn(left, right):
    return lax.dot_general(left, right, (((1,), (0,)), ((), ())), preferred_element_type=F32)


def dot_nt(left, right):
    return lax.dot_general(left, right, (((1,), (1,)), ((), ())), preferred_element_type=F32)


def dot_tn(left, right):
    return lax.dot_general(left, right, (((0,), (0,)), ((), ())), preferred_element_type=F32)


def inverse_rms(rows):
    return lax.rsqrt(jnp.mean(rows * rows, axis=-1, keepdims=True) + EPS)


def loop(count, body):
    def step(index, carry):
        body(index)
        return carry

    lax.fori_loop(0, count, step, 0)


def scratch_plan(count, width, half, rows):
    length = 2 * count
    blocks = (DEPTH, 2, 2, rows, half)
    return dict(
        x=((count, width), F32),
        x2=((count, width), F32),
        cd=((count, width), F32),
        dh=((count, width), F32),
        qf=((length, half), F32),
        h1=((length, width), BF),
        gb=((2, count, width), BF),
        du=((2, count, width), BF),
        ab=((2, count, half), BF),
        abh=((2, length, half), BF),
        of=((2, length, half), BF),
        dos=((count, half), BF),
        dof=((length, half), BF),
        qkv=((3, length, half), BF),
        dq=((2, 3, length, half), BF),
        tz=((2 * DEPTH, 2, rows, count), BF),
        th=((2 * DEPTH, 2, rows, count), BF),
        to=((2 * DEPTH, 2, rows, length), BF),
        tzr=((2 * DEPTH, rows, count), BF),
        thr=((2 * DEPTH, rows, count), BF),
        tor=((2 * DEPTH, rows, length), BF),
        t1=((2 * DEPTH, 2, rows, length), BF),
        t1r=((2 * DEPTH, rows, length), BF),
        bias=((length, length), F32),
        p0=((8, count, count), BF),
        p1=((8, length, count), BF),
        dh1r=((count, width), BF),
        wst=((UNITS, rows, half), F32),
        w=((9,) + blocks, BF),
        s=((8, DEPTH, 2, rows, half), BF),
        yr=((DEPTH, 2, rows, half), BF),
        xr=((7, DEPTH, rows, half), BF),
        zr=((7, DEPTH - 1, rows, half), BF),
        g=((12, rows, half), BF),
        go=((2, rows, half), BF),
        gr=((2, rows, half), BF),
        gn=((DEPTH, 2, 2, rows, 128), BF),
        gs=((128, 128), F32),
        fs=((8, half), F32),
        gt=((8, width), F32),
        dg=((2, 8, width), F32),
        sm=((4, 8, width), F32),
        smr=((3, 8, width), F32),
        smz=((DEPTH, 8, width), F32),
    )


HOPS = 168
ORDER = (
    "gz", "stv", "stk", "sto", "oxv", "stO", "std", "stq", "gx", "stD", "bias", "stup", "gb",
    "fzv1", "gc", "fzv2", "h1", "fzv3", "fcv", "oxk", "fzk1", "fxv", "fzk2", "fzk3", "fck", "oxq",
    "fzq1", "fxk", "fzq2", "h1_", "Pv", "Pk", "fzq3", "oxup", "t1", "fcq", "fzup1", "fxq", "fzup2",
    "fzup3", "zao", "zaO", "zad", "szD", "Pq", "A0", "fxup", "A1", "zio", "A2", "zaD", "A3", "A4",
    "ziO", "A5", "A6", "zbo", "A7", "zid", "so", "fcup", "zbO", "fxo", "zbd", "ziD", "fyup", "fxO",
    "fxd", "x2", "h2", "u", "zbD", "th", "tz", "to", "dz", "dh2", "dx2", "do0", "Wd", "do1", "out",
    "Wup", "axd01", "axd02", "B0", "axd03", "B1", "B2", "axd11", "abc", "B3", "axd12", "B4",
    "axd13", "axd10", "Wo", "B5", "B6", "axo1", "B7", "axo2", "dvk", "dq", "axo3", "axd00", "azd0",
    "ayup", "Wv", "Wk", "axup1", "aed0", "Wq", "axup2", "axo0", "azo", "axup3", "dhp", "dho",
    "aeo", "axv1", "axup0", "azd1", "axv2", "azup", "axv3", "axv0", "axk1", "axk2", "axk3", "azv",
    "ig", "axk0", "aed1", "axq1", "smx", "aeup", "axq2", "aev", "axq3", "azk", "axq0", "smy",
    "aek", "smz", "azq", "sme", "aeq",
)


def layer_kernel(
    names, head_dim, x_hbm, cot_hbm, starts, w_hbm, gains_own, qscale,
    out_hbm, grad_in_hbm, grad_hbm, small_hbm, *scratch
):
    m = types.SimpleNamespace(**dict(zip(names, scratch[: len(names)])))
    send_sems, recv_sems, load_sems, store_sems = scratch[len(names):]
    sems = (send_sems, recv_sems)
    count, width = m.x.shape
    length, half = m.dof.shape
    rows = m.wst.shape[1]
    heads = half // head_dim

    me = lax.axis_index("dp")
    y = lax.axis_index("seq")
    z = lax.div(me, 4)
    x = lax.rem(lax.div(me, 2), 2)
    c = lax.rem(me, 2)
    oy, ox, oc = 1 - y, 1 - x, 1 - c
    to_y = {"seq": oy}
    to_x = {"dp": 4 * z + 2 * ox + c}
    to_c = {"dp": 4 * z + 2 * x + oc}
    up_z = [lax.rem(z + k, DEPTH) for k in range(DEPTH)]
    down_z = [lax.rem(z + DEPTH - k, DEPTH) for k in range(DEPTH)]
    to_z = [{"dp": 4 * up_z[k] + 2 * x + c} for k in range(DEPTH)]
    inner = (z == 1) | (z == 2)
    near_z = z + 1 - 2 * lax.rem(z, 2)
    to_near = {"dp": 4 * near_z + 2 * x + c}
    to_middle = {"dp": 4 * (DEPTH - 1 - z) + 2 * x + c}
    near = pl.ds(2 * lax.div(z, 2), 2)
    far = pl.ds(2 - 2 * lax.div(z, 2), 2)
    hops = []

    def send(source, target, arriving, device, when=None, into=None):
        one = Hop(len(hops), sems, source, target, arriving, device, when, into)
        hops.append(one)
        return one

    own_row = pl.multiple_of(y * count, count)
    peer_row = pl.multiple_of(oy * count, count)

    names_of = ["v", "k", "q", "up", "o", "O", "d", "D"]
    unit_part = [2, 1, 0, 4, 3, 3, 5, 5]
    unit_half = [y, y, y, y, y, oy, y, oy]
    unit_slot = [2, 1, 0, 5 + y, 3 + y, 3 + oy, 7 + y, 7 + oy]
    swap_slot = 5 + oy
    loads = []
    for u in range(UNITS):
        start = pl.multiple_of(unit_part[u] * width + unit_half[u] * half, 128)
        loads.append(
            pltpu.make_async_copy(w_hbm.at[:, pl.ds(start, half)], m.wst.at[u], load_sems.at[u])
        )
        loads[u].start()
    load_x = pltpu.make_async_copy(x_hbm, m.x, load_sems.at[UNITS])
    load_cot = pltpu.make_async_copy(cot_hbm, m.cd, load_sems.at[UNITS + 1])
    load_x.start()
    load_cot.start()
    steps = {}

    def step(name):
        def keep(body):
            steps[name] = body
            return body

        return keep

    barrier = pltpu.get_barrier_semaphore()
    for device in (to_y, to_x, to_c, to_z[1], to_z[2], to_z[3]):
        pl.semaphore_signal(barrier, inc=1, device_id=device, device_id_type=MESH)
    m.gs[...] = jnp.zeros_like(m.gs)
    m.gs[0:2, 0:rows] = gains_own[...]
    m.gn[z, x, c] = jnp.transpose(m.gs[...])[:rows].astype(BF)
    stretch = jnp.maximum(qscale[...], 0.0) + jnp.log1p(jnp.exp(-jnp.abs(qscale[...])))
    m.fs[...] = jnp.zeros_like(m.fs)
    m.fs[0:1, 0:head_dim] = QUERY_BASE / math.sqrt(head_dim) * stretch
    one_head = m.fs[...]
    every = one_head
    for head in range(1, heads):
        every = every + pltpu.roll(one_head, head * head_dim, 1)
    m.fs[...] = every
    factor = m.fs.at[0:1]
    pl.semaphore_wait(barrier, 6)

    hop = {}

    @step("gz")
    def _():
        block = m.gn.at[z, x, c]
        for k in range(1, DEPTH):
            hop["gz", k] = send(block, block, m.gn.at[down_z[k], x, c], to_z[k])

    @step("gx")
    def _():
        for k in range(1, DEPTH):
            hop["gz", k].arrived()
        block = m.gn.at[:, x, c]
        hop["gx"] = send(block, block, m.gn.at[:, ox, c], to_x)

    @step("gc")
    def _():
        hop["gx"].arrived()
        block = m.gn.at[:, :, c]
        hop["gc"] = send(block, block, m.gn.at[:, :, oc], to_c)

    @step("gb")
    def _():
        load_cot.wait()

        def make_gb(index):
            at = pl.ds(index * STEP_ROWS, STEP_ROWS)
            m.gb[0, at] = m.cd[at].astype(BF)

        loop(count // STEP_ROWS, make_gb)
        hop["gb"] = send(m.gb.at[0], m.gb.at[1], m.gb.at[1], to_c)

    @step("bias")
    def _():
        position = lax.broadcasted_iota(jnp.int32, (1, length), 1)
        begin = jnp.zeros((1, length), jnp.int32)
        for j in range(starts.shape[1]):
            begin = jnp.maximum(begin, jnp.where(starts[0, j] <= position, starts[0, j], 0))

        def make_bias(index):
            key = lax.broadcasted_iota(jnp.int32, (STEP_ROWS, length), 0) + index * STEP_ROWS
            kept = (key <= position) & (key >= begin)
            m.bias[pl.ds(index * STEP_ROWS, STEP_ROWS)] = jnp.where(kept, 0.0, NEG)

        loop(length // STEP_ROWS, make_bias)
        m.of[y] = jnp.zeros_like(m.of[y])
        m.dq[0] = jnp.zeros_like(m.dq[0])
        m.dg[...] = jnp.zeros_like(m.dg)

    h1_own, h1_peer = m.h1.at[pl.ds(own_row, count)], m.h1.at[pl.ds(peer_row, count)]

    @step("h1")
    def _():
        load_x.wait()
        hop["gc"].arrived()
        gains = m.gn[...].reshape(width, 128).astype(F32)
        m.gt[...] = jnp.transpose(gains)[:8]

        def make_h1(index):
            values = m.x[pl.ds(index * STEP_ROWS, STEP_ROWS)]
            normed = values * inverse_rms(values)
            at = pl.ds(pl.multiple_of(own_row + index * STEP_ROWS, STEP_ROWS), STEP_ROWS)
            m.h1[at] = (normed * m.gt[0:1]).astype(BF)

        loop(count // STEP_ROWS, make_h1)
        hop["h1"] = send(h1_own, h1_own, h1_peer, to_y)

    def unit_steps(u):
        name, slot = names_of[u], unit_slot[u]

        @step("st" + name)
        def _():
            loads[u].wait()
            m.w[slot, z, x, c] = m.wst[u].astype(BF)
            block = m.w.at[slot, z, x, c]
            for k in range(1, DEPTH):
                hop["z", u, k] = send(block, block, m.w.at[slot, down_z[k], x, c], to_z[k])

        def forward(k):
            def body():
                if k:
                    hop["z", u, k].arrived()
                block = m.w.at[slot, down_z[k], x, c]
                hop["x", u, k] = send(block, block, m.w.at[slot, down_z[k], ox, c], to_x)

            return body

        steps["ox" + name] = forward(0)
        for k in range(1, DEPTH):
            steps[f"fz{name}{k}"] = forward(k)

        @step("fc" + name)
        def _():
            block = m.w.at[slot, :, x, c]
            hop["c", u, 0] = send(block, block, m.w.at[slot, :, x, oc], to_c)

        @step("fx" + name)
        def _():
            for k in range(DEPTH):
                hop["x", u, k].arrived()
            if name == "up":
                block = m.w.at[slot, :, :, c]
                hop["y", u] = send(block, block, m.w.at[swap_slot, :, :, c], to_y)
            block = m.w.at[slot, :, ox, c]
            hop["c", u, 1] = send(block, block, m.w.at[slot, :, ox, oc], to_c)

        @step("fy" + name)
        def _():
            hop["y", u].arrived()
            block = m.w.at[swap_slot, :, :, c]
            hop["yc", u] = send(block, block, m.w.at[swap_slot, :, :, oc], to_c)

    def tree_steps(u, first_x):
        name, slot = names_of[u], unit_slot[u]
        side = slice(None) if first_x else x

        def pair_start():
            block = m.w.at[slot, z, side, c]
            hop["za", u] = send(block, block, m.w.at[slot, near_z, side, c], to_near)

        @step("st" + name)
        def _():
            loads[u].wait()
            m.w[slot, z, x, c] = m.wst[u].astype(BF)
            if first_x:
                block = m.w.at[slot, z, x, c]
                hop["xo", u] = send(block, block, m.w.at[slot, z, ox, c], to_x)
            else:
                pair_start()

        @step("sz" + name)
        def _():
            hop["xo", u].arrived()
            pair_start()

        @step("za" + name)
        def _():
            hop["za", u].arrived()
            block = m.w.at[slot, near, side, c]
            hop["zb", u] = send(
                block, block, m.w.at[slot, far, side, c], to_middle, when=inner
            )
            if not first_x:
                hop["xa", u] = send(block, block, m.w.at[slot, near, ox, c], to_x)

        @step("zi" + name)
        def _():
            pl.when(inner)(hop["zb", u].arrived)
            block = m.w.at[slot, far, side, c]
            hop["zc", u] = send(
                block, block, None, to_near, when=inner, into=hop["zb", u].number
            )

        @step("zb" + name)
        def _():
            pl.when(jnp.logical_not(inner))(hop["zb", u].arrived)
            if first_x:
                block = m.w.at[slot, :, :, c]
                hop["c", u, 1] = send(block, block, m.w.at[slot, :, :, oc], to_c)
                return
            block = m.w.at[slot, far, x, c]
            hop["xb", u] = send(block, block, m.w.at[slot, far, ox, c], to_x)
            block = m.w.at[slot, :, x, c]
            hop["c", u, 0] = send(block, block, m.w.at[slot, :, x, oc], to_c)

        @step("fx" + name)
        def _():
            hop["xa", u].arrived()
            hop["xb", u].arrived()
            block = m.w.at[slot, :, ox, c]
            hop["c", u, 1] = send(block, block, m.w.at[slot, :, ox, oc], to_c)

    for u in range(UNITS):
        if names_of[u] in TREE:
            tree_steps(u, names_of[u] == TREE[-1])
        else:
            unit_steps(u)

    def ready(*wanted):
        for name in wanted:
            u = names_of.index(name)
            if ("c", u, 0) in hop:
                hop["c", u, 0].arrived()
            hop["c", u, 1].arrived()
            if name == "up":
                hop["yc", u].arrived()

    def weight(slot):
        return m.w[slot].reshape(width, half)

    def project(part):
        def block(index):
            at = pl.ds(pl.multiple_of(index * count, count), count)
            result = dot_nn(m.h1[at], weight(part))
            if part == 0:
                m.qf[at] = result
                result = result * factor[...]
            m.qkv[part, at] = result.astype(BF)

        loop(2, block)

    @step("t1")
    def _():
        def transpose_h1(index):
            at = pl.ds(pl.multiple_of(index * count, count), count)
            m.t1[:, :, :, at] = jnp.transpose(m.h1[at]).reshape(2 * DEPTH, 2, rows, count)

        loop(2, transpose_h1)
        hop["t1"] = send(m.t1.at[:, oc], m.t1r, m.t1r, to_c)

    def project_step(name):
        def body():
            ready(name)
            project("qkv".index(name))

        return body

    for name in "qkv":
        steps["P" + name] = project_step(name)

    def head_window(head):
        first = min(head * head_dim // 128 * 128, half - 256)
        lane = lax.broadcasted_iota(jnp.int32, (1, 256), 1) + first
        inside = (lane >= head * head_dim) & (lane < (head + 1) * head_dim)
        return slice(first, first + 256), jnp.where(inside, 1.0, 0.0).astype(BF)

    def attend(head):
        window, mask = head_window(head)
        keys = m.qkv[1, :, window]
        queries = m.qkv[0, :, window] * mask
        values = m.qkv[2, :, window] * mask
        for b in range(2):
            at, upto = slice(b * count, (b + 1) * count), (b + 1) * count
            scores = dot_nt(keys[:upto], queries[at]) + m.bias[:upto, at]
            top = jnp.max(scores, axis=0, keepdims=True)
            expo = jnp.exp(scores - top)
            total = jnp.sum(expo, axis=0, keepdims=True)
            probs = (expo * (1.0 / total)).astype(BF)
            kept = m.p1 if b else m.p0
            kept[head] = probs
            found = dot_tn(probs, values[:upto])
            m.of[y, at, window] = m.of[y, at, window] + found.astype(BF)

    for head in range(heads):
        steps[f"A{head}"] = functools.partial(attend, head)

    own_rows, peer_rows = pl.ds(own_row, count), pl.ds(peer_row, count)

    @step("so")
    def _():
        block = m.of.at[y, peer_rows]
        hop["o"] = send(block, block, m.of.at[oy, own_rows], to_y)
        block = m.of.at[y, own_rows]
        hop["o2"] = send(block, block, m.of.at[oy, peer_rows], to_y)

    @step("to")
    def _():
        hop["o2"].arrived()

        def transpose_o(index):
            m.to[pl.ds(index * DEPTH, DEPTH)] = jnp.transpose(m.of[index]).reshape(
                DEPTH, 2, rows, length
            )

        loop(2, transpose_o)
        hop["to"] = send(m.to.at[:, oc], m.tor, m.tor, to_c)

    def mix(index):
        at = pl.ds(pl.multiple_of(index * half, 128), half)
        right = weight(3 + index)
        m.x2[:, at] = m.x[:, at] + (
            dot_nn(m.of[0, own_rows], right[:half]) + dot_nn(m.of[1, own_rows], right[half:])
        )

    @step("x2")
    def _():
        hop["o"].arrived()
        ready("o", "O")
        loop(2, mix)

    def make_h2(index):
        at = pl.ds(pl.multiple_of(index * STEP_ROWS, STEP_ROWS), STEP_ROWS)
        values = m.x2[at]
        normed = values * inverse_rms(values)
        m.h1[at] = (normed * m.gt[1:2]).astype(BF)

    h2, act = m.h1.at[pl.ds(0, count)], m.h1.at[pl.ds(count, count)]

    @step("h2")
    def _():
        hop["h1"].left()
        loop(count // STEP_ROWS, make_h2)

    @step("th")
    def _():
        m.th[...] = jnp.transpose(h2[...]).reshape(2 * DEPTH, 2, rows, count)
        hop["th"] = send(m.th.at[:, oc], m.thr, m.thr, to_c)

    def back(left, slot, index):
        at = pl.ds(2 * index, 2)
        return dot_nt(left[0], m.w[slot, at].reshape(half, half)) + dot_nt(
            left[1], m.w[slot + 1, at].reshape(half, half)
        )

    def halves(whole_rows):
        return whole_rows[:, :half], whole_rows[:, half:]

    def feed(index):
        at = pl.ds(pl.multiple_of(index * half, 128), half)
        gate = dot_nn(h2[...], weight(5 + index))
        m.dh[:, at] = gate
        act[:, at] = (gate / (1.0 + jnp.exp(-gate))).astype(BF)

    @step("u")
    def _():
        ready("up")
        loop(2, feed)

    @step("tz")
    def _():
        m.tz[...] = jnp.transpose(act[...]).reshape(2 * DEPTH, 2, rows, count)
        hop["tz"] = send(m.tz.at[:, oc], m.tzr, m.tzr, to_c)

    def gate_back(index):
        at = pl.ds(pl.multiple_of(index * half, 128), half)
        gate = m.dh[:, at]
        sigma = 1.0 / (1.0 + jnp.exp(-gate))
        grad = back(halves(m.gb[0]), 7, index)
        m.du[0, :, at] = (grad * sigma * (1.0 + gate * (1.0 - sigma))).astype(BF)

    @step("dz")
    def _():
        ready("d", "D")
        loop(2, gate_back)
        hop["du"] = send(m.du.at[0], m.du.at[1], m.du.at[1], to_c)

    def weight_grad(slot, here, there, rights):
        def block(index):
            right_here, right_there = rights()
            at = pl.ds(DEPTH * index, DEPTH)
            depth = here.shape[-1]
            total = dot_nn(here[at, c].reshape(DEPTH * rows, depth), right_here)
            total = total + dot_nn(there[at].reshape(DEPTH * rows, depth), right_there)
            m.s[slot, pl.ds(2 * index, 2)] = total.astype(BF).reshape(2, 2, rows, half)

        loop(2, block)

    def column_grad(first, here, there, right):
        def one(index):
            at = pl.ds(pl.multiple_of(index * half, 128), half)
            weight_grad(first + index, here, there, lambda: (right[0, :, at], right[1, :, at]))

        loop(2, one)

    sum_names = ["q", "k", "v", "o", "up", "d0", "d1"]
    sum_slot = [0, 1, 2, 3, 4 + y, 6, 7]
    whole = {5: 0, 6: 1}
    columns = [0, 2, 4, 6, 8, 10, 11]

    def start_x(name):
        u = sum_names.index(name)
        for k in (1, 2, 3, 0):
            target = m.xr.at[u, up_z[k]]
            hop["sx", u, k] = send(m.s.at[sum_slot[u], up_z[k], ox], target, target, to_x)

    @step("ayup")
    def _():
        hop["sy"].arrived()
        slot = sum_slot[4]

        def block(index):
            for k in range(2):
                total = m.s[slot, index, k].astype(F32) + m.yr[index, k].astype(F32)
                m.s[slot, index, k] = total.astype(BF)

        loop(DEPTH, block)
        start_x("up")

    def sum_steps(u):
        name, slot = sum_names[u], sum_slot[u]

        def add_x(k):
            def body():
                hop["sx", u, k].arrived()
                target = up_z[k]
                total = m.s[slot, target, x].astype(F32) + m.xr[u, target].astype(F32)
                m.s[slot, target, x] = total.astype(BF)
                if k:
                    there = m.zr.at[u, k - 1]
                    hop["sz", u, k] = send(m.s.at[slot, target, x], there, there, to_z[k])

            return body

        for k in range(DEPTH):
            steps[f"ax{name}{k}"] = add_x(k)

        @step("az" + name)
        def _():
            total = m.s[slot, z, x].astype(F32)
            for k in range(1, DEPTH):
                hop["sz", u, k].arrived()
                total = total + m.zr[u, k - 1].astype(F32)
            if u in whole:
                mine, other = m.go.at[whole[u]], m.gr.at[whole[u]]
                mine[...] = total.astype(BF)
                hop["se", u] = send(mine, other, other, to_y)
            else:
                mine, other = m.g.at[columns[u] + y], m.g.at[columns[u] + oy]
                mine[...] = total.astype(BF)
                hop["se", u] = send(mine, mine, other, to_y)

        @step("ae" + name)
        def _():
            hop["se", u].arrived()
            ready_columns = [columns[u]]
            if u in whole:
                total = m.go[whole[u]].astype(F32) + m.gr[whole[u]].astype(F32)
                m.g[columns[u]] = total.astype(BF)
            else:
                ready_columns.append(columns[u] + 1)
            for column in ready_columns:
                store(m.g.at[column], grad_hbm.at[:, pl.ds(column * half, half)])

    for u in range(len(sum_names)):
        sum_steps(u)

    stores = []

    def store(source, target):
        copy = pltpu.make_async_copy(source, target, store_sems.at[len(stores)])
        copy.start()
        stores.append(copy)

    @step("Wd")
    def _():
        hop["tz"].arrived()
        hop["gb"].arrived()
        column_grad(6, m.tz, m.tzr, m.gb)
        start_x("d0")
        start_x("d1")

    @step("Wup")
    def _():
        hop["th"].arrived()
        hop["du"].arrived()
        column_grad(4, m.th, m.thr, m.du)
        hop["sy"] = send(m.s.at[4 + oy], m.yr, m.yr, to_y)

    @step("Wo")
    def _():
        hop["to"].arrived()
        hop["abc"].arrived()
        weight_grad(3, m.to, m.tor, lambda: (m.abh[0], m.abh[1]))
        start_x("o")

    def feed_back(index):
        at = pl.ds(pl.multiple_of(index * half, 128), half)
        m.dh[:, at] = back(halves(m.du[0]), 5, index)

    @step("dh2")
    def _():
        loop(2, feed_back)

    def norm_back(values, inverse, gain, grad):
        normed = values * inverse
        scaled = grad * gain
        mean = jnp.mean(scaled * normed, axis=-1, keepdims=True)
        part = jnp.sum((grad * normed).reshape(STEP_ROWS // 8, 8, width), axis=0)
        return inverse * (scaled - normed * mean), part

    def make_dx2(index):
        at = pl.ds(pl.multiple_of(index * STEP_ROWS, STEP_ROWS), STEP_ROWS)
        values = m.x2[at]
        grad, part = norm_back(values, inverse_rms(values), m.gt[1:2], m.dh[at])
        m.dg[1] = m.dg[1] + part
        total = m.cd[at] + grad
        m.cd[at] = total
        m.ab[0, at], m.ab[1, at] = halves(total.astype(BF))

    @step("dx2")
    def _():
        loop(count // STEP_ROWS, make_dx2)

    @step("do0")
    def _():
        m.dos[...] = back((m.ab[0], m.ab[1]), 3, oy).astype(BF)
        target, arriving = m.dof.at[pl.ds(own_row, count)], m.dof.at[pl.ds(peer_row, count)]
        hop["do"] = send(m.dos, target, arriving, to_y)
        m.abh[0, own_rows] = m.ab[y]
        target, arriving = m.abh.at[0, own_rows], m.abh.at[0, peer_rows]
        hop["ab"] = send(m.ab.at[oy], target, arriving, to_y)

    @step("abc")
    def _():
        hop["ab"].arrived()
        hop["abc"] = send(m.abh.at[0], m.abh.at[1], m.abh.at[1], to_c)

    @step("do1")
    def _():
        m.dof[pl.ds(own_row, count)] = back((m.ab[0], m.ab[1]), 3, y).astype(BF)

    def finish_out(index):
        at = pl.ds(pl.multiple_of(index * half, 128), half)
        m.x2[:, at] = m.x2[:, at] + dot_nn(act[...], weight(7 + index))

    @step("out")
    def _():
        loop(2, finish_out)
        store(m.x2, out_hbm)

    def attend_back(head):
        window, mask = head_window(head)
        masked_keys = m.qkv[1, :, window] * mask
        queries = m.qkv[0, :, window] * mask
        values = m.qkv[2, :, window]
        grads = m.dof[:, window] * mask
        key_sum, value_sum = None, None
        for b in (1, 0):
            at, upto = slice(b * count, (b + 1) * count), (b + 1) * count
            low_probs = m.p1[head] if b else m.p0[head]
            probs = low_probs.astype(F32)
            grad_probs = dot_nt(values[:upto], grads[at])
            inner = jnp.sum(probs * grad_probs, axis=0, keepdims=True)
            low = (probs * (grad_probs - inner)).astype(BF)
            grad_query = dot_tn(low, masked_keys[:upto])
            m.dq[0, 0, at, window] = m.dq[0, 0, at, window] + grad_query.astype(BF)
            value_part = dot_nn(low_probs, grads[at])
            key_part = dot_nn(low, queries[at])
            if b:
                key_sum, value_sum = key_part[:count], value_part[:count]
                later = slice(count, length)
                m.dq[0, 1, later, window] = m.dq[0, 1, later, window] + key_part[count:].astype(BF)
                m.dq[0, 2, later, window] = m.dq[0, 2, later, window] + value_part[count:].astype(BF)
            else:
                m.dq[0, 1, at, window] = m.dq[0, 1, at, window] + (key_sum + key_part).astype(BF)
                m.dq[0, 2, at, window] = m.dq[0, 2, at, window] + (value_sum + value_part).astype(BF)

    def attend_back_step(head):
        def body():
            if head == 0:
                hop["do"].arrived()
            attend_back(head)

        return body

    for head in range(heads):
        steps[f"B{head}"] = attend_back_step(head)

    def share(part):
        hop["d", part] = send(m.dq.at[0, part], m.dq.at[1, part], m.dq.at[1, part], to_c)

    @step("dvk")
    def _():
        share(2)
        share(1)

    def scale_query(index):
        at = pl.ds(pl.multiple_of(index * STEP_ROWS, STEP_ROWS), STEP_ROWS)
        values = m.dq[0, 0, at].astype(F32)
        part = (values * m.qf[at]).reshape(STEP_ROWS // 8, 8, half)
        m.dg[0, :, :half] = m.dg[0, :, :half] + jnp.sum(part, axis=0)
        m.dq[0, 0, at] = (values * factor[...]).astype(BF)

    @step("dq")
    def _():
        loop(length // STEP_ROWS, scale_query)
        share(0)
        m.sm[0] = jnp.zeros_like(m.sm[0])
        m.sm[0, 2:3] = jnp.sum(m.dg[0], axis=0, keepdims=True)
        m.dg[0] = jnp.zeros_like(m.dg[0])

    def attention_weight(name):
        part = "qkv".index(name)

        def body():
            if name == "v":
                hop["t1"].arrived()
            hop["d", part].arrived()
            weight_grad(part, m.t1, m.t1r, lambda: (m.dq[0, part], m.dq[1, part]))
            start_x(name)

        return body

    for name in "qkv":
        steps["W" + name] = attention_weight(name)

    def hidden_back(row, index):
        at = pl.ds(2 * index, 2)
        total = None
        for part in range(3):
            term = dot_nt(
                m.dq[0, part, pl.ds(row, count)], m.w[part, at].reshape(half, half)
            )
            total = term if total is None else total + term
        return total

    def hidden_peer(index):
        at = pl.ds(pl.multiple_of(index * half, 128), half)
        h2[:, at] = hidden_back(peer_row, index).astype(BF)

    def hidden_own(index):
        at = pl.ds(pl.multiple_of(index * half, 128), half)
        m.dh[:, at] = hidden_back(own_row, index)

    @step("dhp")
    def _():
        loop(2, hidden_peer)
        hop["dh"] = send(h2, m.dh1r, m.dh1r, to_y)

    @step("dho")
    def _():
        loop(2, hidden_own)

    def make_input_grad(index):
        at = pl.ds(pl.multiple_of(index * STEP_ROWS, STEP_ROWS), STEP_ROWS)
        values = m.x[at]
        grad = m.dh[at] + m.dh1r[at].astype(F32)
        grad, part = norm_back(values, inverse_rms(values), m.gt[0:1], grad)
        m.dg[0] = m.dg[0] + part
        m.cd[at] = m.cd[at] + grad

    @step("ig")
    def _():
        hop["dh"].arrived()
        loop(count // STEP_ROWS, make_input_grad)
        store(m.cd, grad_in_hbm)
        for g in range(2):
            m.sm[0, g:g + 1] = jnp.sum(m.dg[g], axis=0, keepdims=True)
        hop["smc"] = send(m.sm.at[0], m.smr.at[0], m.smr.at[0], to_c)

    @step("smx")
    def _():
        hop["smc"].arrived()
        m.sm[1] = m.sm[0] + m.smr[0]
        hop["smx"] = send(m.sm.at[1], m.smr.at[1], m.smr.at[1], to_x)

    @step("smy")
    def _():
        hop["smx"].arrived()
        m.sm[2] = m.sm[1] + m.smr[1]
        hop["smy"] = send(m.sm.at[2], m.smr.at[2], m.smr.at[2], to_y)

    @step("smz")
    def _():
        hop["smy"].arrived()
        m.smz[z] = m.sm[2] + m.smr[2]
        block = m.smz.at[z]
        for k in range(1, DEPTH):
            hop["smz", k] = send(block, block, m.smz.at[down_z[k]], to_z[k])

    @step("sme")
    def _():
        for k in range(1, DEPTH):
            hop["smz", k].arrived()
        total = ((m.smz[0] + m.smz[1]) + m.smz[2]) + m.smz[3]
        m.sm[3] = total
        m.gs[0:8] = pltpu.roll(total, lax.rem(width - me * rows, width), 1)[:, :128]
        folded = m.sm[3, 2:3, 0:half]
        part = folded
        for head in range(1, heads):
            part = part + pltpu.roll(folded, half - head * head_dim, 1)
        m.gs[2:3] = part[:, :128]
        store(m.gs.at[0:8], small_hbm)

    for name in ORDER:
        if name == "h1_":
            hop["h1"].arrived()
        else:
            steps[name]()
    for one in hops:
        one.left()
    for copy in stores:
        copy.wait()


def fits(count, groups, owners, width, head_dim, rows):
    half = width // groups
    return (
        groups == 2
        and owners == 4 * DEPTH
        and count % 128 == 0
        and count % STEP_ROWS == 0
        and rows % 16 == 0
        and rows == width // owners
        and half % 128 == 0
        and half >= 256
        and half % head_dim == 0
        and (half // head_dim) % 4 == 0
        and head_dim <= 128
    )


def fused_layer(
    inputs,
    cotangent,
    starts,
    weights,
    weight_m,
    weight_v,
    gains,
    gain_m,
    gain_v,
    qscale,
    qscale_m,
    qscale_v,
):
    count, width = inputs.shape[1:]
    head_dim = width // HEADS
    groups = lax.axis_size("seq")
    half = width // groups
    rows, columns = weights.shape
    plan = scratch_plan(count, width, half, rows)
    anywhere = pl.BlockSpec(memory_space=pl.ANY)
    inside = pl.BlockSpec(memory_space=pltpu.VMEM)
    outputs, input_grad, grads, small = pl.pallas_call(
        functools.partial(layer_kernel, tuple(plan), head_dim),
        out_shape=(
            jax.ShapeDtypeStruct((count, width), F32),
            jax.ShapeDtypeStruct((count, width), F32),
            jax.ShapeDtypeStruct((rows, columns), BF),
            jax.ShapeDtypeStruct((8, 128), F32),
        ),
        in_specs=[
            anywhere,
            anywhere,
            pl.BlockSpec(memory_space=pltpu.SMEM),
            anywhere,
            inside,
            inside,
        ],
        out_specs=(anywhere,) * 4,
        scratch_shapes=[pltpu.VMEM(shape, kind) for shape, kind in plan.values()]
        + [
            pltpu.SemaphoreType.DMA((HOPS,)),
            pltpu.SemaphoreType.DMA((HOPS,)),
            pltpu.SemaphoreType.DMA((UNITS + 2,)),
            pltpu.SemaphoreType.DMA((15,)),
        ],
        compiler_params=pltpu.CompilerParams(
            collective_id=0, has_side_effects=True, vmem_limit_bytes=VMEM_BYTES
        ),
    )(inputs[0], cotangent[0], starts, weights, gains, qscale[None])
    steps = 5
    block = pl.BlockSpec((rows, columns // steps), lambda index: (0, index))
    pair = pl.BlockSpec((2, rows), lambda index: (0, 0))
    single = pl.BlockSpec((1, head_dim), lambda index: (0, 0))
    tokens = pl.BlockSpec((count, width // steps), lambda index: (0, index))
    matrix = jax.ShapeDtypeStruct((rows, columns), F32)
    result = pl.pallas_call(
        update_kernel,
        grid=(steps,),
        out_shape=(outputs, input_grad, matrix, matrix, matrix)
        + (jax.ShapeDtypeStruct((rows, columns), BF),)
        + (gains,) * 3
        + (jax.ShapeDtypeStruct((1, head_dim), F32),) * 3,
        in_specs=[tokens, tokens, block, pl.BlockSpec((8, 128), lambda index: (0, 0))]
        + [block] * 3
        + [pair] * 3
        + [single] * 3,
        out_specs=(tokens, tokens) + (block,) * 4 + (pair,) * 3 + (single,) * 3,
        compiler_params=pltpu.CompilerParams(vmem_limit_bytes=VMEM_BYTES),
    )(
        outputs, input_grad, grads, small, weights, weight_m, weight_v, gains, gain_m, gain_v,
        qscale[None], qscale_m[None], qscale_v[None],
    )
    return (result[0][None], result[1][None]) + tuple(result[2:9]) + tuple(
        value[0] for value in result[9:]
    )


def update_kernel(
    outputs, input_grad, grads, small, weights, weight_m, weight_v, gains, gain_m, gain_v,
    qscale, qscale_m, qscale_v, outputs_new, input_grad_new, weights_new, weight_m_new,
    weight_v_new, weights_low, gains_new, gain_m_new, gain_v_new, qscale_new, qscale_m_new,
    qscale_v_new
):
    outputs_new[...] = outputs[...]
    input_grad_new[...] = input_grad[...]
    head_dim = qscale.shape[1]

    @pl.when(pl.program_id(0) == 0)
    def _():
        gains_new[...], gain_m_new[...], gain_v_new[...] = adamw(
            gains[...], small[0:2, : gains.shape[1]], gain_m[...], gain_v[...], RATE_GAIN
        )
        slope = QUERY_BASE / math.sqrt(head_dim) / (1.0 + jnp.exp(-qscale[...]))
        qscale_new[...], qscale_m_new[...], qscale_v_new[...] = adamw(
            qscale[...], small[2:3, :head_dim] * slope, qscale_m[...], qscale_v[...], RATE_GAIN
        )

    updated, weight_m_new[...], weight_v_new[...] = adamw(
        weights[...], grads[...].astype(F32), weight_m[...], weight_v[...], RATE_MATRIX
    )
    weights_new[...] = updated
    weights_low[...] = updated.astype(BF)


def on_device(*arrays):
    count, width = arrays[0].shape[1:]
    rows = arrays[3].shape[0]
    if fits(count, lax.axis_size("seq"), lax.axis_size("dp"), width, width // HEADS, rows):
        return fused_layer(*arrays)
    return plain_layer(*arrays)


def solution(mesh):
    placed = (
        P("dp", "seq", None),
        P("dp", "seq", None),
        P("dp", None),
        P("dp", None),
        P("dp", None),
        P("dp", None),
        P(None, "dp"),
        P(None, "dp"),
        P(None, "dp"),
        P(),
        P(),
        P(),
    )
    return jax.shard_map(
        on_device,
        mesh=mesh,
        in_specs=placed,
        out_specs=placed[:2] + placed[3:6] + placed[5:],
        check_vma=False,
    )
```

```python
import functools
import math
import types

import jax
import jax.numpy as jnp
from jax import lax
from jax.experimental import pallas as pl
from jax.experimental.pallas import tpu as pltpu
from jax.sharding import PartitionSpec as P

HEADS = 16
STEP = 10


EPS = 1e-06
QUERY_BASE = 1.442695
BETA_ONE = 0.5
BETA_TWO = 0.5
ADAM_EPS = 1e-08
RATE_MATRIX = 0.02
RATE_GAIN = 0.3
DECAY = 0.1
NEG = -1e30


def norm_forward(values, gain):
    inverse = lax.rsqrt(jnp.mean(values * values, axis=-1, keepdims=True) + EPS)
    normed = values * inverse
    return (normed, inverse, (normed * gain).astype(jnp.bfloat16))


def norm_backward(grad, normed, inverse, gain):
    gain_grad = jnp.sum(grad * normed, axis=0)
    scaled = grad * gain
    return (
        inverse * (scaled - normed * jnp.mean(scaled * normed, axis=-1, keepdims=True)),
        gain_grad,
    )


def adamw(param, grad, first, second, rate):
    first_new = BETA_ONE * first + (1.0 - BETA_ONE) * grad
    second_new = BETA_TWO * second + (1.0 - BETA_TWO) * grad * grad
    first_hat = first_new / (1.0 - BETA_ONE**STEP)
    second_hat = second_new / (1.0 - BETA_TWO**STEP)
    param_new = param - rate * (first_hat / (jnp.sqrt(second_hat) + ADAM_EPS) + DECAY * param)
    return (param_new, first_new, second_new)


def plain_layer(
    inputs,
    cotangent,
    starts,
    weights,
    weight_m,
    weight_v,
    gains,
    gain_m,
    gain_v,
    qscale,
    qscale_m,
    qscale_v,
):
    full_w, full_g = (
        lax.all_gather(weights.astype(jnp.bfloat16), "dp", axis=0, tiled=True),
        lax.all_gather(gains.astype(jnp.bfloat16), "dp", axis=1, tiled=True),
    )
    width = full_w.shape[0]
    head_dim = width // HEADS
    w_qkv = full_w[:, : 3 * width]
    w_out = full_w[:, 3 * width : 4 * width]
    w_up = full_w[:, 4 * width : 5 * width]
    w_down = full_w[:, 5 * width :]
    gain_one = full_g[0].astype(jnp.float32)
    gain_two = full_g[1].astype(jnp.float32)
    resid = inputs[0]
    count = resid.shape[0]
    groups = lax.axis_size("seq")
    length = count * groups
    local_width = width // groups
    local_heads = local_width // head_dim
    block = min(512, length)
    blocks = length // block
    normed_one, inverse_one, hidden_one = norm_forward(resid, gain_one)
    projected = jnp.dot(hidden_one, w_qkv, preferred_element_type=jnp.float32).reshape(
        count, 3, width
    )
    base_scale = QUERY_BASE / math.sqrt(head_dim)
    tiled = jnp.tile(base_scale * jax.nn.softplus(qscale), HEADS)
    factor = jnp.stack([tiled, jnp.ones_like(tiled), jnp.ones_like(tiled)])
    outgoing = (projected * factor[None]).astype(jnp.bfloat16)
    arrived = lax.all_to_all(outgoing, "seq", split_axis=2, concat_axis=0, tiled=True)
    queries = arrived[:, 0].reshape(length, local_heads, head_dim)
    keys = arrived[:, 1].reshape(length, local_heads, head_dim)
    values = arrived[:, 2].reshape(length, local_heads, head_dim)
    positions = jnp.arange(length, dtype=jnp.int32)
    segment = jnp.sum((positions[:, None] >= starts[0][None, :]).astype(jnp.int32), axis=1) - 1

    def masked_scores(start):
        query_block = lax.dynamic_slice_in_dim(queries, start, block, 0)
        raw = jnp.einsum("qhd,khd->hqk", query_block, keys, preferred_element_type=jnp.float32)
        rows = start + jnp.arange(block, dtype=jnp.int32)
        row_seg = lax.dynamic_slice_in_dim(segment, start, block, 0)
        allowed = (positions[None, :] <= rows[:, None]) & (segment[None, :] == row_seg[:, None])
        return (query_block, jnp.where(allowed[None], raw, NEG))

    def forward_block(index):
        query_block, masked = masked_scores(index * block)
        top = jnp.max(masked, axis=-1, keepdims=True)
        expo = jnp.exp(masked - top)
        total = jnp.sum(expo, axis=-1, keepdims=True)
        probs = (expo / total).astype(jnp.bfloat16)
        attended = jnp.einsum("hqk,khd->qhd", probs, values, preferred_element_type=jnp.float32)
        return (attended.astype(jnp.bfloat16), (top + jnp.log(total))[..., 0])

    head_out, log_totals = lax.map(forward_block, jnp.arange(blocks, dtype=jnp.int32))
    head_out = head_out.reshape(length, local_width)
    attn_rows = lax.all_to_all(head_out, "seq", split_axis=0, concat_axis=1, tiled=True)
    mixed = resid + jnp.dot(attn_rows, w_out, preferred_element_type=jnp.float32)
    normed_two, inverse_two, hidden_two = norm_forward(mixed, gain_two)
    gate = jnp.dot(hidden_two, w_up, preferred_element_type=jnp.float32)
    sigma = jax.nn.sigmoid(gate)
    activ = (gate * sigma).astype(jnp.bfloat16)
    outputs = mixed + jnp.dot(activ, w_down, preferred_element_type=jnp.float32)
    grad_top = cotangent[0]
    grad_low = grad_top.astype(jnp.bfloat16)
    grad_activ = jnp.dot(grad_low, w_down.T, preferred_element_type=jnp.float32)
    grad_gate = (grad_activ * sigma * (1.0 + gate * (1.0 - sigma))).astype(jnp.bfloat16)
    grad_down = jnp.dot(activ.T, grad_low, preferred_element_type=jnp.float32)
    grad_up = jnp.dot(hidden_two.T, grad_gate, preferred_element_type=jnp.float32)
    grad_hidden_two = jnp.dot(grad_gate, w_up.T, preferred_element_type=jnp.float32)
    grad_norm_two, gain_grad_two = norm_backward(grad_hidden_two, normed_two, inverse_two, gain_two)
    grad_mixed = grad_top + grad_norm_two
    mixed_low = grad_mixed.astype(jnp.bfloat16)
    grad_out = jnp.dot(attn_rows.T, mixed_low, preferred_element_type=jnp.float32)
    grad_attn = jnp.dot(mixed_low, w_out.T, preferred_element_type=jnp.float32).astype(jnp.bfloat16)
    grad_heads = lax.all_to_all(grad_attn, "seq", split_axis=1, concat_axis=0, tiled=True).reshape(
        length, local_heads, head_dim
    )

    def backward_block(carry, index):
        key_sum, value_sum = carry
        start = index * block
        query_block, masked = masked_scores(start)
        grad_block = lax.dynamic_slice_in_dim(grad_heads, start, block, 0)
        lse_block = log_totals[index]
        probs = jnp.exp(masked - lse_block[:, :, None])
        value_sum = value_sum + jnp.einsum(
            "hqk,qhd->khd",
            probs.astype(jnp.bfloat16),
            grad_block,
            preferred_element_type=jnp.float32,
        )
        grad_probs = jnp.einsum(
            "qhd,khd->hqk", grad_block, values, preferred_element_type=jnp.float32
        )
        grad_scores = probs * (grad_probs - jnp.sum(probs * grad_probs, axis=-1, keepdims=True))
        scores_low = grad_scores.astype(jnp.bfloat16)
        grad_query = jnp.einsum(
            "hqk,khd->qhd", scores_low, keys, preferred_element_type=jnp.float32
        )
        key_sum = key_sum + jnp.einsum(
            "hqk,qhd->khd", scores_low, query_block, preferred_element_type=jnp.float32
        )
        return ((key_sum, value_sum), grad_query)

    empty = jnp.zeros((length, local_heads, head_dim), jnp.float32)
    (key_grad, value_grad), query_grad = lax.scan(
        backward_block, (empty, empty), jnp.arange(blocks, dtype=jnp.int32)
    )
    stacked = jnp.stack(
        [
            query_grad.reshape(length, local_width),
            key_grad.reshape(length, local_width),
            value_grad.reshape(length, local_width),
        ],
        axis=1,
    ).astype(jnp.bfloat16)
    returned = lax.all_to_all(stacked, "seq", split_axis=0, concat_axis=2, tiled=True)
    scaled_grad = returned[:, 0].astype(jnp.float32)
    scale_part = jnp.sum(scaled_grad * projected[:, 0], axis=0).reshape(HEADS, head_dim).sum(axis=0)
    query_low = (scaled_grad * tiled[None]).astype(jnp.bfloat16)
    grad_qkv_rows = jnp.concatenate([query_low[:, None], returned[:, 1:]], axis=1).reshape(
        count, 3 * width
    )
    grad_qkv = jnp.dot(hidden_one.T, grad_qkv_rows, preferred_element_type=jnp.float32)
    grad_hidden_one = jnp.dot(grad_qkv_rows, w_qkv.T, preferred_element_type=jnp.float32)
    grad_norm_one, gain_grad_one = norm_backward(grad_hidden_one, normed_one, inverse_one, gain_one)
    input_grad = grad_mixed + grad_norm_one
    all_grads = jnp.concatenate([grad_qkv, grad_out, grad_up, grad_down], axis=1)
    gain_grads = jnp.stack([gain_grad_one, gain_grad_two])
    owned_w, owned_g = (
        lax.psum_scatter(
            all_grads.astype(jnp.bfloat16), "dp", scatter_dimension=0, tiled=True
        ).astype(jnp.float32),
        lax.psum_scatter(
            gain_grads.astype(jnp.bfloat16), "dp", scatter_dimension=1, tiled=True
        ).astype(jnp.float32),
    )
    owned_w, owned_g = (
        lax.psum(owned_w.astype(jnp.bfloat16), "seq").astype(jnp.float32),
        lax.psum(owned_g.astype(jnp.bfloat16), "seq").astype(jnp.float32),
    )
    scale_grad = lax.psum(scale_part, ("dp", "seq")) * base_scale * jax.nn.sigmoid(qscale)
    weights_new, weight_m_new, weight_v_new = adamw(
        weights, owned_w, weight_m, weight_v, RATE_MATRIX
    )
    gains_new, gain_m_new, gain_v_new = adamw(gains, owned_g, gain_m, gain_v, RATE_GAIN)
    qscale_new, qscale_m_new, qscale_v_new = adamw(
        qscale, scale_grad, qscale_m, qscale_v, RATE_GAIN
    )
    return (
        outputs[None],
        input_grad[None],
        weights_new,
        weight_m_new,
        weight_v_new,
        weights_new.astype(jnp.bfloat16),
        gains_new,
        gain_m_new,
        gain_v_new,
        qscale_new,
        qscale_m_new,
        qscale_v_new,
    )


MESH = pl.DeviceIdType.MESH
BF = jnp.bfloat16
F32 = jnp.float32
DEPTH = 4
STEP_ROWS = 32
UNITS = 8
FIRST_X = ("d", "D")
VMEM_BYTES = 64 * 1024 * 1024


class Hop:
    def __init__(self, number, sems, source, target, arriving, device, when=None, into=None):
        self.number, self.when, self.pending = number, when, True
        self.out = self.describe(number, into or number, sems, source, target, device)
        if arriving is not None:
            self.back = self.describe(number, number, sems, arriving, arriving, device)
        self.guard(self.out.start)

    @staticmethod
    def describe(number, into, sems, source, target, device):
        return pltpu.make_async_remote_copy(
            src_ref=source,
            dst_ref=target,
            send_sem=sems[0].at[number],
            recv_sem=sems[1].at[into],
            device_id=device,
            device_id_type=MESH,
        )

    def guard(self, action):
        if self.when is None:
            action()
        else:
            pl.when(self.when)(action)

    def arrived(self):
        self.back.wait_recv()

    def left(self):
        if self.pending:
            self.guard(self.out.wait_send)
        self.pending = False


def dot_nn(left, right):
    return lax.dot_general(left, right, (((1,), (0,)), ((), ())), preferred_element_type=F32)


def dot_nt(left, right):
    return lax.dot_general(left, right, (((1,), (1,)), ((), ())), preferred_element_type=F32)


def dot_tn(left, right):
    return lax.dot_general(left, right, (((0,), (0,)), ((), ())), preferred_element_type=F32)


def inverse_rms(rows):
    return lax.rsqrt(jnp.mean(rows * rows, axis=-1, keepdims=True) + EPS)


def loop(count, body):
    def step(index, carry):
        body(index)
        return carry

    lax.fori_loop(0, count, step, 0)


def scratch_plan(count, width, half, rows):
    length = 2 * count
    blocks = (DEPTH, 2, 2, rows, half)
    return dict(
        x=((count, width), F32),
        x2=((count, width), F32),
        cd=((count, width), F32),
        dh=((count, width), F32),
        qf=((length, half), F32),
        h1=((length, width), BF),
        gb=((2, count, width), BF),
        du=((2, count, width), BF),
        ab=((2, count, half), BF),
        abh=((2, length, half), BF),
        of=((2, length, half), BF),
        dos=((count, half), BF),
        dof=((length, half), BF),
        qkv=((3, length, half), BF),
        dq=((2, 3, length, half), BF),
        tz=((2 * DEPTH, 2, rows, count), BF),
        th=((2 * DEPTH, 2, rows, count), BF),
        to=((2 * DEPTH, 2, rows, length), BF),
        tzr=((2 * DEPTH, rows, count), BF),
        thr=((2 * DEPTH, rows, count), BF),
        tor=((2 * DEPTH, rows, length), BF),
        t1=((2 * DEPTH, 2, rows, length), BF),
        t1r=((2 * DEPTH, rows, length), BF),
        bias=((3 * count, count), F32),
        p0=((8, count, count), BF),
        p1=((8, length, count), BF),
        dh1r=((count, width), BF),
        wst=((UNITS, rows, half), F32),
        w=((9,) + blocks, BF),
        s=((8, DEPTH, 2, rows, half), BF),
        yr=((DEPTH, 2, rows, half), BF),
        xr=((7, DEPTH, rows, half), BF),
        zr=((7, DEPTH - 1, rows, half), BF),
        g=((12, rows, half), BF),
        go=((2, rows, half), BF),
        gr=((2, rows, half), BF),
        gn=((DEPTH, 2, 2, rows, 128), BF),
        gs=((128, 128), F32),
        fs=((8, half), F32),
        gt=((8, width), F32),
        dg=((2, 8, width), F32),
        sm=((4, 8, width), F32),
        smr=((3, 8, width), F32),
        smz=((DEPTH, 8, width), F32),
    )


HOPS = 176
ORDER = (
    "gz", "stup", "stD", "stk", "stv", "stq", "stO", "bias", "sto", "std", "gb", "gx", "zaup",
    "gc", "zav", "ziup", "h1", "ziv", "zbup", "zak", "zbv", "zaq", "zik", "fxup", "h1_", "t1",
    "ziq", "zbk", "zao", "zbq", "zaO", "szd", "fxv", "zio", "Pv", "ziO", "zad", "szD", "fyup",
    "zbo", "fxk", "zbO", "zid", "Pk", "zaD", "fxq", "Pq", "A0", "A1", "A2", "A3", "A4", "A5",
    "ziD", "A6", "A7", "so", "zbd", "fxo", "fxO", "zbD", "x2", "h2", "th", "u", "tz", "dz", "dh2",
    "dx2", "Wd", "do0", "do1", "out", "to", "axd01", "Wup", "axd02", "axd03", "B0", "B1", "B2",
    "B3", "B4", "axd11", "B5", "B6", "B7", "dvk", "dq", "axd12", "abc", "axd00", "azd0", "axd13",
    "Wv", "axd10", "Wk", "Wq", "dhp", "axv1", "dho", "Wo", "azd1", "axv2", "axv3", "axv0", "ayup",
    "axk1", "aed0", "azv", "axk2", "axk3", "axk0", "axq1", "azk", "axq2", "ig", "axq3", "aed1",
    "axq0", "smx", "aev", "axo1", "aek", "azq", "axo2", "axo3", "aeq", "axo0", "axup1", "azo",
    "axup2", "axup3", "aeo", "axup0", "smy", "smz", "azup", "sme", "aeup",
)


def layer_kernel(
    names, head_dim, x_hbm, cot_hbm, starts, w_hbm, gains_own, qscale,
    out_hbm, grad_in_hbm, grad_hbm, small_hbm, *scratch
):
    m = types.SimpleNamespace(**dict(zip(names, scratch[: len(names)])))
    send_sems, recv_sems, load_sems, store_sems = scratch[len(names):]
    sems = (send_sems, recv_sems)
    count, width = m.x.shape
    length, half = m.dof.shape
    rows = m.wst.shape[1]
    heads = half // head_dim

    me = lax.axis_index("dp")
    y = lax.axis_index("seq")
    z = lax.div(me, 4)
    x = lax.rem(lax.div(me, 2), 2)
    c = lax.rem(me, 2)
    oy, ox, oc = 1 - y, 1 - x, 1 - c
    to_y = {"seq": oy}
    to_x = {"dp": 4 * z + 2 * ox + c}
    to_c = {"dp": 4 * z + 2 * x + oc}
    up_z = [lax.rem(z + k, DEPTH) for k in range(DEPTH)]
    down_z = [lax.rem(z + DEPTH - k, DEPTH) for k in range(DEPTH)]
    to_z = [{"dp": 4 * up_z[k] + 2 * x + c} for k in range(DEPTH)]
    inner = (z == 1) | (z == 2)
    near_z = z + 1 - 2 * lax.rem(z, 2)
    to_near = {"dp": 4 * near_z + 2 * x + c}
    to_middle = {"dp": 4 * (DEPTH - 1 - z) + 2 * x + c}
    outer = jnp.logical_not(inner)
    near_first = 2 * lax.div(z, 2)
    far_first = 2 - near_first
    near, far = pl.ds(near_first, 2), pl.ds(far_first, 2)
    hops = []

    def send(source, target, arriving, device, when=None, into=None):
        one = Hop(len(hops), sems, source, target, arriving, device, when, into)
        hops.append(one)
        return one

    own_row = pl.multiple_of(y * count, count)
    peer_row = pl.multiple_of(oy * count, count)

    names_of = ["v", "k", "q", "up", "o", "O", "d", "D"]
    unit_part = [2, 1, 0, 4, 3, 3, 5, 5]
    unit_half = [y, y, y, y, y, oy, y, oy]
    unit_slot = [2, 1, 0, 5 + y, 3 + y, 3 + oy, 7 + y, 7 + oy]
    swap_slot = 5 + oy
    loads = []
    for u in range(UNITS):
        start = pl.multiple_of(unit_part[u] * width + unit_half[u] * half, 128)
        loads.append(
            pltpu.make_async_copy(w_hbm.at[:, pl.ds(start, half)], m.wst.at[u], load_sems.at[u])
        )
        loads[u].start()
    load_x = pltpu.make_async_copy(x_hbm, m.x, load_sems.at[UNITS])
    load_cot = pltpu.make_async_copy(cot_hbm, m.cd, load_sems.at[UNITS + 1])
    load_x.start()
    load_cot.start()
    steps = {}

    def step(name):
        def keep(body):
            steps[name] = body
            return body

        return keep

    barrier = pltpu.get_barrier_semaphore()
    for device in (to_y, to_x, to_c, to_z[1], to_z[2], to_z[3]):
        pl.semaphore_signal(barrier, inc=1, device_id=device, device_id_type=MESH)
    m.gs[...] = jnp.zeros_like(m.gs)
    m.gs[0:2, 0:rows] = gains_own[...]
    m.gn[z, x, c] = jnp.transpose(m.gs[...])[:rows].astype(BF)
    stretch = jnp.maximum(qscale[...], 0.0) + jnp.log1p(jnp.exp(-jnp.abs(qscale[...])))
    m.fs[...] = jnp.zeros_like(m.fs)
    m.fs[0:1, 0:head_dim] = QUERY_BASE / math.sqrt(head_dim) * stretch
    one_head = m.fs[...]
    every = one_head
    for head in range(1, heads):
        every = every + pltpu.roll(one_head, head * head_dim, 1)
    m.fs[...] = every
    factor = m.fs.at[0:1]
    pl.semaphore_wait(barrier, 6)

    hop = {}

    @step("gz")
    def _():
        block = m.gn.at[z, x, c]
        for k in range(1, DEPTH):
            hop["gz", k] = send(block, block, m.gn.at[down_z[k], x, c], to_z[k])

    @step("gx")
    def _():
        for k in range(1, DEPTH):
            hop["gz", k].arrived()
        block = m.gn.at[:, x, c]
        hop["gx"] = send(block, block, m.gn.at[:, ox, c], to_x)

    @step("gc")
    def _():
        hop["gx"].arrived()
        block = m.gn.at[:, :, c]
        hop["gc"] = send(block, block, m.gn.at[:, :, oc], to_c)

    @step("gb")
    def _():
        load_cot.wait()

        def make_gb(index):
            at = pl.ds(index * STEP_ROWS, STEP_ROWS)
            m.gb[0, at] = m.cd[at].astype(BF)

        loop(count // STEP_ROWS, make_gb)
        hop["gb"] = send(m.gb.at[0], m.gb.at[1], m.gb.at[1], to_c)

    @step("bias")
    def _():
        def make_bias(first, offset):
            position = lax.broadcasted_iota(jnp.int32, (1, count), 1) + first
            begin = jnp.zeros((1, count), jnp.int32)
            for j in range(starts.shape[1]):
                begin = jnp.maximum(begin, jnp.where(starts[0, j] <= position, starts[0, j], 0))

            def fill(index):
                key = lax.broadcasted_iota(jnp.int32, (STEP_ROWS, count), 0) + index * STEP_ROWS
                kept = (key <= position) & (key >= begin)
                at = pl.ds(pl.multiple_of(offset + index * STEP_ROWS, STEP_ROWS), STEP_ROWS)
                m.bias[at] = jnp.where(kept, 0.0, NEG)

            loop((first + count) // STEP_ROWS, fill)

        make_bias(0, 0)
        make_bias(count, count)
        m.of[y] = jnp.zeros_like(m.of[y])
        m.dq[0] = jnp.zeros_like(m.dq[0])
        m.dg[...] = jnp.zeros_like(m.dg)

    h1_own, h1_peer = m.h1.at[pl.ds(own_row, count)], m.h1.at[pl.ds(peer_row, count)]

    @step("h1")
    def _():
        load_x.wait()
        hop["gc"].arrived()
        gains = m.gn[...].reshape(width, 128).astype(F32)
        m.gt[...] = jnp.transpose(gains)[:8]

        def make_h1(index):
            values = m.x[pl.ds(index * STEP_ROWS, STEP_ROWS)]
            normed = values * inverse_rms(values)
            at = pl.ds(pl.multiple_of(own_row + index * STEP_ROWS, STEP_ROWS), STEP_ROWS)
            m.h1[at] = (normed * m.gt[0:1]).astype(BF)

        loop(count // STEP_ROWS, make_h1)
        hop["h1"] = send(h1_own, h1_own, h1_peer, to_y)

    def unit_steps(u, first_x):
        name, slot = names_of[u], unit_slot[u]
        side = slice(None) if first_x else x

        def pair_start():
            block = m.w.at[slot, z, side, c]
            hop["za", u] = send(block, block, m.w.at[slot, near_z, side, c], to_near)

        @step("st" + name)
        def _():
            loads[u].wait()
            m.w[slot, z, x, c] = m.wst[u].astype(BF)
            if first_x:
                block = m.w.at[slot, z, x, c]
                hop["xo", u] = send(block, block, m.w.at[slot, z, ox, c], to_x)
            else:
                pair_start()

        @step("sz" + name)
        def _():
            hop["xo", u].arrived()
            pair_start()

        @step("za" + name)
        def _():
            hop["za", u].arrived()
            block = m.w.at[slot, near, side, c]
            hop["zb", u] = send(
                block, block, m.w.at[slot, far, side, c], to_middle, when=inner
            )
            if not first_x:
                hop["xa", u] = send(block, block, m.w.at[slot, near, ox, c], to_x)

        @step("zi" + name)
        def _():
            pl.when(inner)(hop["zb", u].arrived)
            block = m.w.at[slot, far, side, c]
            hop["zc", u] = send(
                block, block, None, to_near, when=inner, into=hop["zb", u].number
            )

        @step("zb" + name)
        def _():
            pl.when(outer)(hop["zb", u].arrived)
            if first_x:
                block = m.w.at[slot, :, :, c]
                hop["c", u, 1] = send(block, block, m.w.at[slot, :, :, oc], to_c)
                return
            block = m.w.at[slot, far, x, c]
            hop["xb", u] = send(block, block, m.w.at[slot, far, ox, c], to_x)
            block = m.w.at[slot, :, x, c]
            hop["c", u, 0] = send(block, block, m.w.at[slot, :, x, oc], to_c)

        @step("fx" + name)
        def _():
            hop["xa", u].arrived()
            hop["xb", u].arrived()
            if name == "up":
                block = m.w.at[slot, :, :, c]
                hop["y", u] = send(block, block, m.w.at[swap_slot, :, :, c], to_y)
            block = m.w.at[slot, :, ox, c]
            hop["c", u, 1] = send(block, block, m.w.at[slot, :, ox, oc], to_c)

        @step("fy" + name)
        def _():
            hop["y", u].arrived()
            block = m.w.at[swap_slot, :, :, c]
            hop["yc", u] = send(block, block, m.w.at[swap_slot, :, :, oc], to_c)

    for u in range(UNITS):
        unit_steps(u, names_of[u] in FIRST_X)

    def ready(*wanted):
        for name in wanted:
            u = names_of.index(name)
            if ("c", u, 0) in hop:
                hop["c", u, 0].arrived()
            hop["c", u, 1].arrived()
            if name == "up":
                hop["yc", u].arrived()

    def weight(slot):
        return m.w[slot].reshape(width, half)

    def project(part):
        def block(index):
            at = pl.ds(pl.multiple_of(index * count, count), count)
            result = dot_nn(m.h1[at], weight(part))
            if part == 0:
                m.qf[at] = result
                result = result * factor[...]
            m.qkv[part, at] = result.astype(BF)

        loop(2, block)

    @step("t1")
    def _():
        def transpose_h1(index):
            at = pl.ds(pl.multiple_of(index * count, count), count)
            m.t1[:, :, :, at] = jnp.transpose(m.h1[at]).reshape(2 * DEPTH, 2, rows, count)

        loop(2, transpose_h1)
        hop["t1"] = send(m.t1.at[:, oc], m.t1r, m.t1r, to_c)

    def project_step(name):
        def body():
            ready(name)
            project("qkv".index(name))

        return body

    for name in "qkv":
        steps["P" + name] = project_step(name)

    def head_window(head):
        first = min(head * head_dim // 128 * 128, half - 256)
        lane = lax.broadcasted_iota(jnp.int32, (1, 256), 1) + first
        inside = (lane >= head * head_dim) & (lane < (head + 1) * head_dim)
        return slice(first, first + 256), jnp.where(inside, 1.0, 0.0).astype(BF)

    def attend(head):
        window, mask = head_window(head)
        keys = m.qkv[1, :, window]
        queries = m.qkv[0, :, window] * mask
        values = m.qkv[2, :, window] * mask
        for b in range(2):
            at, upto = slice(b * count, (b + 1) * count), (b + 1) * count
            allowed = m.bias[pl.ds(b * count, upto)]
            scores = dot_nt(keys[:upto], queries[at]) + allowed
            top = jnp.max(scores, axis=0, keepdims=True)
            expo = jnp.exp(scores - top)
            total = jnp.sum(expo, axis=0, keepdims=True)
            probs = (expo * (1.0 / total)).astype(BF)
            kept = m.p1 if b else m.p0
            kept[head] = probs
            found = dot_tn(probs, values[:upto])
            m.of[y, at, window] = m.of[y, at, window] + found.astype(BF)

    for head in range(heads):
        steps[f"A{head}"] = functools.partial(attend, head)

    own_rows, peer_rows = pl.ds(own_row, count), pl.ds(peer_row, count)

    @step("so")
    def _():
        block = m.of.at[y, peer_rows]
        hop["o"] = send(block, block, m.of.at[oy, own_rows], to_y)
        block = m.of.at[y, own_rows]
        hop["o2"] = send(block, block, m.of.at[oy, peer_rows], to_y)

    @step("to")
    def _():
        hop["o2"].arrived()

        def transpose_o(index):
            m.to[pl.ds(index * DEPTH, DEPTH)] = jnp.transpose(m.of[index]).reshape(
                DEPTH, 2, rows, length
            )

        loop(2, transpose_o)
        hop["to"] = send(m.to.at[:, oc], m.tor, m.tor, to_c)

    def mix(index):
        at = pl.ds(pl.multiple_of(index * half, 128), half)
        right = weight(3 + index)
        m.x2[:, at] = m.x[:, at] + (
            dot_nn(m.of[0, own_rows], right[:half]) + dot_nn(m.of[1, own_rows], right[half:])
        )

    @step("x2")
    def _():
        hop["o"].arrived()
        ready("o", "O")
        loop(2, mix)

    def make_h2(index):
        at = pl.ds(pl.multiple_of(index * STEP_ROWS, STEP_ROWS), STEP_ROWS)
        values = m.x2[at]
        normed = values * inverse_rms(values)
        m.h1[at] = (normed * m.gt[1:2]).astype(BF)

    h2, act = m.h1.at[pl.ds(0, count)], m.h1.at[pl.ds(count, count)]

    @step("h2")
    def _():
        hop["h1"].left()
        loop(count // STEP_ROWS, make_h2)

    @step("th")
    def _():
        m.th[...] = jnp.transpose(h2[...]).reshape(2 * DEPTH, 2, rows, count)
        hop["th"] = send(m.th.at[:, oc], m.thr, m.thr, to_c)

    def back(left, slot, index):
        at = pl.ds(2 * index, 2)
        return dot_nt(left[0], m.w[slot, at].reshape(half, half)) + dot_nt(
            left[1], m.w[slot + 1, at].reshape(half, half)
        )

    def halves(whole_rows):
        return whole_rows[:, :half], whole_rows[:, half:]

    def feed(index):
        at = pl.ds(pl.multiple_of(index * half, 128), half)
        gate = dot_nn(h2[...], weight(5 + index))
        m.dh[:, at] = gate
        act[:, at] = (gate / (1.0 + jnp.exp(-gate))).astype(BF)

    @step("u")
    def _():
        ready("up")
        loop(2, feed)

    @step("tz")
    def _():
        m.tz[...] = jnp.transpose(act[...]).reshape(2 * DEPTH, 2, rows, count)
        hop["tz"] = send(m.tz.at[:, oc], m.tzr, m.tzr, to_c)

    def gate_back(index):
        at = pl.ds(pl.multiple_of(index * half, 128), half)
        gate = m.dh[:, at]
        sigma = 1.0 / (1.0 + jnp.exp(-gate))
        grad = back(halves(m.gb[0]), 7, index)
        m.du[0, :, at] = (grad * sigma * (1.0 + gate * (1.0 - sigma))).astype(BF)

    @step("dz")
    def _():
        ready("d", "D")
        loop(2, gate_back)
        hop["du"] = send(m.du.at[0], m.du.at[1], m.du.at[1], to_c)

    def weight_grad(slot, here, there, rights):
        def block(index):
            right_here, right_there = rights()
            at = pl.ds(DEPTH * index, DEPTH)
            depth = here.shape[-1]
            total = dot_nn(here[at, c].reshape(DEPTH * rows, depth), right_here)
            total = total + dot_nn(there[at].reshape(DEPTH * rows, depth), right_there)
            m.s[slot, pl.ds(2 * index, 2)] = total.astype(BF).reshape(2, 2, rows, half)

        loop(2, block)

    def column_grad(first, here, there, right):
        def one(index):
            at = pl.ds(pl.multiple_of(index * half, 128), half)
            weight_grad(first + index, here, there, lambda: (right[0, :, at], right[1, :, at]))

        loop(2, one)

    sum_names = ["q", "k", "v", "o", "up", "d0", "d1"]
    sum_slot = [0, 1, 2, 3, 4 + y, 6, 7]
    whole = {5: 0, 6: 1}
    columns = [0, 2, 4, 6, 8, 10, 11]

    def start_x(name):
        u = sum_names.index(name)
        for k in (1, 2, 3, 0):
            target = m.xr.at[u, up_z[k]]
            hop["sx", u, k] = send(m.s.at[sum_slot[u], up_z[k], ox], target, target, to_x)

    @step("ayup")
    def _():
        hop["sy"].arrived()
        slot = sum_slot[4]

        def block(index):
            for k in range(2):
                total = m.s[slot, index, k].astype(F32) + m.yr[index, k].astype(F32)
                m.s[slot, index, k] = total.astype(BF)

        loop(DEPTH, block)
        start_x("up")

    def sum_steps(u):
        name, slot = sum_names[u], sum_slot[u]

        def add_x(k):
            def body():
                hop["sx", u, k].arrived()
                target = up_z[k]
                total = m.s[slot, target, x].astype(F32) + m.xr[u, target].astype(F32)
                m.s[slot, target, x] = total.astype(BF)
                if k:
                    there = m.zr.at[u, k - 1]
                    hop["sz", u, k] = send(m.s.at[slot, target, x], there, there, to_z[k])

            return body

        for k in range(DEPTH):
            steps[f"ax{name}{k}"] = add_x(k)

        @step("az" + name)
        def _():
            total = m.s[slot, z, x].astype(F32)
            for k in range(1, DEPTH):
                hop["sz", u, k].arrived()
                total = total + m.zr[u, k - 1].astype(F32)
            if u in whole:
                mine, other = m.go.at[whole[u]], m.gr.at[whole[u]]
                mine[...] = total.astype(BF)
                hop["se", u] = send(mine, other, other, to_y)
            else:
                mine, other = m.g.at[columns[u] + y], m.g.at[columns[u] + oy]
                mine[...] = total.astype(BF)
                hop["se", u] = send(mine, mine, other, to_y)

        @step("ae" + name)
        def _():
            hop["se", u].arrived()
            ready_columns = [columns[u]]
            if u in whole:
                total = m.go[whole[u]].astype(F32) + m.gr[whole[u]].astype(F32)
                m.g[columns[u]] = total.astype(BF)
            else:
                ready_columns.append(columns[u] + 1)
            for column in ready_columns:
                store(m.g.at[column], grad_hbm.at[:, pl.ds(column * half, half)])

    for u in range(len(sum_names)):
        sum_steps(u)

    stores = []

    def store(source, target):
        copy = pltpu.make_async_copy(source, target, store_sems.at[len(stores)])
        copy.start()
        stores.append(copy)

    @step("Wd")
    def _():
        hop["tz"].arrived()
        hop["gb"].arrived()
        column_grad(6, m.tz, m.tzr, m.gb)
        start_x("d0")
        start_x("d1")

    @step("Wup")
    def _():
        hop["th"].arrived()
        hop["du"].arrived()
        column_grad(4, m.th, m.thr, m.du)
        hop["sy"] = send(m.s.at[4 + oy], m.yr, m.yr, to_y)

    @step("Wo")
    def _():
        hop["to"].arrived()
        hop["abc"].arrived()
        weight_grad(3, m.to, m.tor, lambda: (m.abh[0], m.abh[1]))
        start_x("o")

    def feed_back(index):
        at = pl.ds(pl.multiple_of(index * half, 128), half)
        m.dh[:, at] = back(halves(m.du[0]), 5, index)

    @step("dh2")
    def _():
        loop(2, feed_back)

    def norm_back(values, inverse, gain, grad):
        normed = values * inverse
        scaled = grad * gain
        mean = jnp.mean(scaled * normed, axis=-1, keepdims=True)
        part = jnp.sum((grad * normed).reshape(STEP_ROWS // 8, 8, width), axis=0)
        return inverse * (scaled - normed * mean), part

    def make_dx2(index):
        at = pl.ds(pl.multiple_of(index * STEP_ROWS, STEP_ROWS), STEP_ROWS)
        values = m.x2[at]
        grad, part = norm_back(values, inverse_rms(values), m.gt[1:2], m.dh[at])
        m.dg[1] = m.dg[1] + part
        total = m.cd[at] + grad
        m.cd[at] = total
        m.ab[0, at], m.ab[1, at] = halves(total.astype(BF))

    @step("dx2")
    def _():
        loop(count // STEP_ROWS, make_dx2)

    @step("do0")
    def _():
        m.dos[...] = back((m.ab[0], m.ab[1]), 3, oy).astype(BF)
        target, arriving = m.dof.at[pl.ds(own_row, count)], m.dof.at[pl.ds(peer_row, count)]
        hop["do"] = send(m.dos, target, arriving, to_y)
        m.abh[0, own_rows] = m.ab[y]
        target, arriving = m.abh.at[0, own_rows], m.abh.at[0, peer_rows]
        hop["ab"] = send(m.ab.at[oy], target, arriving, to_y)

    @step("abc")
    def _():
        hop["ab"].arrived()
        hop["abc"] = send(m.abh.at[0], m.abh.at[1], m.abh.at[1], to_c)

    @step("do1")
    def _():
        m.dof[pl.ds(own_row, count)] = back((m.ab[0], m.ab[1]), 3, y).astype(BF)

    def finish_out(index):
        at = pl.ds(pl.multiple_of(index * half, 128), half)
        m.x2[:, at] = m.x2[:, at] + dot_nn(act[...], weight(7 + index))

    @step("out")
    def _():
        loop(2, finish_out)
        store(m.x2, out_hbm)

    def attend_back(head):
        window, mask = head_window(head)
        masked_keys = m.qkv[1, :, window] * mask
        queries = m.qkv[0, :, window] * mask
        values = m.qkv[2, :, window]
        grads = m.dof[:, window] * mask
        key_sum, value_sum = None, None
        for b in (1, 0):
            at, upto = slice(b * count, (b + 1) * count), (b + 1) * count
            low_probs = m.p1[head] if b else m.p0[head]
            probs = low_probs.astype(F32)
            grad_probs = dot_nt(values[:upto], grads[at])
            inner = jnp.sum(probs * grad_probs, axis=0, keepdims=True)
            low = (probs * (grad_probs - inner)).astype(BF)
            grad_query = dot_tn(low, masked_keys[:upto])
            m.dq[0, 0, at, window] = m.dq[0, 0, at, window] + grad_query.astype(BF)
            value_part = dot_nn(low_probs, grads[at])
            key_part = dot_nn(low, queries[at])
            if b:
                key_sum, value_sum = key_part[:count], value_part[:count]
                later = slice(count, length)
                m.dq[0, 1, later, window] = m.dq[0, 1, later, window] + key_part[count:].astype(BF)
                m.dq[0, 2, later, window] = m.dq[0, 2, later, window] + value_part[count:].astype(BF)
            else:
                m.dq[0, 1, at, window] = m.dq[0, 1, at, window] + (key_sum + key_part).astype(BF)
                m.dq[0, 2, at, window] = m.dq[0, 2, at, window] + (value_sum + value_part).astype(BF)

    def attend_back_step(head):
        def body():
            if head == 0:
                hop["do"].arrived()
            attend_back(head)

        return body

    for head in range(heads):
        steps[f"B{head}"] = attend_back_step(head)

    def share(part):
        hop["d", part] = send(m.dq.at[0, part], m.dq.at[1, part], m.dq.at[1, part], to_c)

    @step("dvk")
    def _():
        share(2)
        share(1)

    def scale_query(index):
        at = pl.ds(pl.multiple_of(index * STEP_ROWS, STEP_ROWS), STEP_ROWS)
        values = m.dq[0, 0, at].astype(F32)
        part = (values * m.qf[at]).reshape(STEP_ROWS // 8, 8, half)
        m.dg[0, :, :half] = m.dg[0, :, :half] + jnp.sum(part, axis=0)
        m.dq[0, 0, at] = (values * factor[...]).astype(BF)

    @step("dq")
    def _():
        loop(length // STEP_ROWS, scale_query)
        share(0)
        m.sm[0] = jnp.zeros_like(m.sm[0])
        m.sm[0, 2:3] = jnp.sum(m.dg[0], axis=0, keepdims=True)
        m.dg[0] = jnp.zeros_like(m.dg[0])

    def attention_weight(name):
        part = "qkv".index(name)

        def body():
            if name == "v":
                hop["t1"].arrived()
            hop["d", part].arrived()
            weight_grad(part, m.t1, m.t1r, lambda: (m.dq[0, part], m.dq[1, part]))
            start_x(name)

        return body

    for name in "qkv":
        steps["W" + name] = attention_weight(name)

    def hidden_back(row, index):
        at = pl.ds(2 * index, 2)
        total = None
        for part in range(3):
            term = dot_nt(
                m.dq[0, part, pl.ds(row, count)], m.w[part, at].reshape(half, half)
            )
            total = term if total is None else total + term
        return total

    def hidden_peer(index):
        at = pl.ds(pl.multiple_of(index * half, 128), half)
        h2[:, at] = hidden_back(peer_row, index).astype(BF)

    def hidden_own(index):
        at = pl.ds(pl.multiple_of(index * half, 128), half)
        m.dh[:, at] = hidden_back(own_row, index)

    @step("dhp")
    def _():
        loop(2, hidden_peer)
        hop["dh"] = send(h2, m.dh1r, m.dh1r, to_y)

    @step("dho")
    def _():
        loop(2, hidden_own)

    def make_input_grad(index):
        at = pl.ds(pl.multiple_of(index * STEP_ROWS, STEP_ROWS), STEP_ROWS)
        values = m.x[at]
        grad = m.dh[at] + m.dh1r[at].astype(F32)
        grad, part = norm_back(values, inverse_rms(values), m.gt[0:1], grad)
        m.dg[0] = m.dg[0] + part
        m.cd[at] = m.cd[at] + grad

    @step("ig")
    def _():
        hop["dh"].arrived()
        loop(count // STEP_ROWS, make_input_grad)
        store(m.cd, grad_in_hbm)
        for g in range(2):
            m.sm[0, g:g + 1] = jnp.sum(m.dg[g], axis=0, keepdims=True)
        hop["smc"] = send(m.sm.at[0], m.smr.at[0], m.smr.at[0], to_c)

    @step("smx")
    def _():
        hop["smc"].arrived()
        m.sm[1] = m.sm[0] + m.smr[0]
        hop["smx"] = send(m.sm.at[1], m.smr.at[1], m.smr.at[1], to_x)

    @step("smy")
    def _():
        hop["smx"].arrived()
        m.sm[2] = m.sm[1] + m.smr[1]
        hop["smy"] = send(m.sm.at[2], m.smr.at[2], m.smr.at[2], to_y)

    @step("smz")
    def _():
        hop["smy"].arrived()
        m.smz[z] = m.sm[2] + m.smr[2]
        block = m.smz.at[z]
        for k in range(1, DEPTH):
            hop["smz", k] = send(block, block, m.smz.at[down_z[k]], to_z[k])

    @step("sme")
    def _():
        for k in range(1, DEPTH):
            hop["smz", k].arrived()
        total = ((m.smz[0] + m.smz[1]) + m.smz[2]) + m.smz[3]
        m.sm[3] = total
        m.gs[0:8] = pltpu.roll(total, lax.rem(width - me * rows, width), 1)[:, :128]
        folded = m.sm[3, 2:3, 0:half]
        part = folded
        for head in range(1, heads):
            part = part + pltpu.roll(folded, half - head * head_dim, 1)
        m.gs[2:3] = part[:, :128]
        store(m.gs.at[0:8], small_hbm)

    for name in ORDER:
        if name == "h1_":
            hop["h1"].arrived()
        else:
            steps[name]()
    for one in hops:
        one.left()
    for copy in stores:
        copy.wait()


def fits(count, groups, owners, width, head_dim, rows):
    half = width // groups
    return (
        groups == 2
        and owners == 4 * DEPTH
        and count % 128 == 0
        and count % STEP_ROWS == 0
        and rows % 16 == 0
        and rows == width // owners
        and half % 128 == 0
        and half >= 256
        and half % head_dim == 0
        and (half // head_dim) % 4 == 0
        and head_dim <= 128
    )


def fused_layer(
    inputs,
    cotangent,
    starts,
    weights,
    weight_m,
    weight_v,
    gains,
    gain_m,
    gain_v,
    qscale,
    qscale_m,
    qscale_v,
):
    count, width = inputs.shape[1:]
    head_dim = width // HEADS
    groups = lax.axis_size("seq")
    half = width // groups
    rows, columns = weights.shape
    plan = scratch_plan(count, width, half, rows)
    anywhere = pl.BlockSpec(memory_space=pl.ANY)
    inside = pl.BlockSpec(memory_space=pltpu.VMEM)
    outputs, input_grad, grads, small = pl.pallas_call(
        functools.partial(layer_kernel, tuple(plan), head_dim),
        out_shape=(
            jax.ShapeDtypeStruct((count, width), F32),
            jax.ShapeDtypeStruct((count, width), F32),
            jax.ShapeDtypeStruct((rows, columns), BF),
            jax.ShapeDtypeStruct((8, 128), F32),
        ),
        in_specs=[
            anywhere,
            anywhere,
            pl.BlockSpec(memory_space=pltpu.SMEM),
            anywhere,
            inside,
            inside,
        ],
        out_specs=(anywhere,) * 4,
        scratch_shapes=[pltpu.VMEM(shape, kind) for shape, kind in plan.values()]
        + [
            pltpu.SemaphoreType.DMA((HOPS,)),
            pltpu.SemaphoreType.DMA((HOPS,)),
            pltpu.SemaphoreType.DMA((UNITS + 2,)),
            pltpu.SemaphoreType.DMA((15,)),
        ],
        compiler_params=pltpu.CompilerParams(
            collective_id=0, has_side_effects=True, vmem_limit_bytes=VMEM_BYTES
        ),
    )(inputs[0], cotangent[0], starts, weights, gains, qscale[None])
    steps = 5
    block = pl.BlockSpec((rows, columns // steps), lambda index: (0, index))
    pair = pl.BlockSpec((2, rows), lambda index: (0, 0))
    single = pl.BlockSpec((1, head_dim), lambda index: (0, 0))
    tokens = pl.BlockSpec((count, width // steps), lambda index: (0, index))
    matrix = jax.ShapeDtypeStruct((rows, columns), F32)
    result = pl.pallas_call(
        update_kernel,
        grid=(steps,),
        out_shape=(outputs, input_grad, matrix, matrix, matrix)
        + (jax.ShapeDtypeStruct((rows, columns), BF),)
        + (gains,) * 3
        + (jax.ShapeDtypeStruct((1, head_dim), F32),) * 3,
        in_specs=[tokens, tokens, block, pl.BlockSpec((8, 128), lambda index: (0, 0))]
        + [block] * 3
        + [pair] * 3
        + [single] * 3,
        out_specs=(tokens, tokens) + (block,) * 4 + (pair,) * 3 + (single,) * 3,
        compiler_params=pltpu.CompilerParams(vmem_limit_bytes=VMEM_BYTES),
    )(
        outputs, input_grad, grads, small, weights, weight_m, weight_v, gains, gain_m, gain_v,
        qscale[None], qscale_m[None], qscale_v[None],
    )
    return (result[0][None], result[1][None]) + tuple(result[2:9]) + tuple(
        value[0] for value in result[9:]
    )


def update_kernel(
    outputs, input_grad, grads, small, weights, weight_m, weight_v, gains, gain_m, gain_v,
    qscale, qscale_m, qscale_v, outputs_new, input_grad_new, weights_new, weight_m_new,
    weight_v_new, weights_low, gains_new, gain_m_new, gain_v_new, qscale_new, qscale_m_new,
    qscale_v_new
):
    outputs_new[...] = outputs[...]
    input_grad_new[...] = input_grad[...]
    head_dim = qscale.shape[1]

    @pl.when(pl.program_id(0) == 0)
    def _():
        gains_new[...], gain_m_new[...], gain_v_new[...] = adamw(
            gains[...], small[0:2, : gains.shape[1]], gain_m[...], gain_v[...], RATE_GAIN
        )
        slope = QUERY_BASE / math.sqrt(head_dim) / (1.0 + jnp.exp(-qscale[...]))
        qscale_new[...], qscale_m_new[...], qscale_v_new[...] = adamw(
            qscale[...], small[2:3, :head_dim] * slope, qscale_m[...], qscale_v[...], RATE_GAIN
        )

    updated, weight_m_new[...], weight_v_new[...] = adamw(
        weights[...], grads[...].astype(F32), weight_m[...], weight_v[...], RATE_MATRIX
    )
    weights_new[...] = updated
    weights_low[...] = updated.astype(BF)


def on_device(*arrays):
    count, width = arrays[0].shape[1:]
    rows = arrays[3].shape[0]
    if fits(count, lax.axis_size("seq"), lax.axis_size("dp"), width, width // HEADS, rows):
        return fused_layer(*arrays)
    return plain_layer(*arrays)


def solution(mesh):
    placed = (
        P("dp", "seq", None),
        P("dp", "seq", None),
        P("dp", None),
        P("dp", None),
        P("dp", None),
        P("dp", None),
        P(None, "dp"),
        P(None, "dp"),
        P(None, "dp"),
        P(),
        P(),
        P(),
    )
    return jax.shard_map(
        on_device,
        mesh=mesh,
        in_specs=placed,
        out_specs=placed[:2] + placed[3:6] + placed[5:],
        check_vma=False,
    )
```

```python
import functools
import math
import types

import jax
import jax.numpy as jnp
from jax import lax
from jax.experimental import pallas as pl
from jax.experimental.pallas import tpu as pltpu
from jax.sharding import PartitionSpec as P

HEADS = 16
STEP = 10


EPS = 1e-06
QUERY_BASE = 1.442695
BETA_ONE = 0.5
BETA_TWO = 0.5
ADAM_EPS = 1e-08
RATE_MATRIX = 0.02
RATE_GAIN = 0.3
DECAY = 0.1
NEG = -1e30


def norm_forward(values, gain):
    inverse = lax.rsqrt(jnp.mean(values * values, axis=-1, keepdims=True) + EPS)
    normed = values * inverse
    return (normed, inverse, (normed * gain).astype(jnp.bfloat16))


def norm_backward(grad, normed, inverse, gain):
    gain_grad = jnp.sum(grad * normed, axis=0)
    scaled = grad * gain
    return (
        inverse * (scaled - normed * jnp.mean(scaled * normed, axis=-1, keepdims=True)),
        gain_grad,
    )


def adamw(param, grad, first, second, rate):
    first_new = BETA_ONE * first + (1.0 - BETA_ONE) * grad
    second_new = BETA_TWO * second + (1.0 - BETA_TWO) * grad * grad
    first_hat = first_new / (1.0 - BETA_ONE**STEP)
    second_hat = second_new / (1.0 - BETA_TWO**STEP)
    param_new = param - rate * (first_hat / (jnp.sqrt(second_hat) + ADAM_EPS) + DECAY * param)
    return (param_new, first_new, second_new)


def plain_layer(
    inputs,
    cotangent,
    starts,
    weights,
    weight_m,
    weight_v,
    gains,
    gain_m,
    gain_v,
    qscale,
    qscale_m,
    qscale_v,
):
    full_w, full_g = (
        lax.all_gather(weights.astype(jnp.bfloat16), "dp", axis=0, tiled=True),
        lax.all_gather(gains.astype(jnp.bfloat16), "dp", axis=1, tiled=True),
    )
    width = full_w.shape[0]
    head_dim = width // HEADS
    w_qkv = full_w[:, : 3 * width]
    w_out = full_w[:, 3 * width : 4 * width]
    w_up = full_w[:, 4 * width : 5 * width]
    w_down = full_w[:, 5 * width :]
    gain_one = full_g[0].astype(jnp.float32)
    gain_two = full_g[1].astype(jnp.float32)
    resid = inputs[0]
    count = resid.shape[0]
    groups = lax.axis_size("seq")
    length = count * groups
    local_width = width // groups
    local_heads = local_width // head_dim
    block = min(512, length)
    blocks = length // block
    normed_one, inverse_one, hidden_one = norm_forward(resid, gain_one)
    projected = jnp.dot(hidden_one, w_qkv, preferred_element_type=jnp.float32).reshape(
        count, 3, width
    )
    base_scale = QUERY_BASE / math.sqrt(head_dim)
    tiled = jnp.tile(base_scale * jax.nn.softplus(qscale), HEADS)
    factor = jnp.stack([tiled, jnp.ones_like(tiled), jnp.ones_like(tiled)])
    outgoing = (projected * factor[None]).astype(jnp.bfloat16)
    arrived = lax.all_to_all(outgoing, "seq", split_axis=2, concat_axis=0, tiled=True)
    queries = arrived[:, 0].reshape(length, local_heads, head_dim)
    keys = arrived[:, 1].reshape(length, local_heads, head_dim)
    values = arrived[:, 2].reshape(length, local_heads, head_dim)
    positions = jnp.arange(length, dtype=jnp.int32)
    segment = jnp.sum((positions[:, None] >= starts[0][None, :]).astype(jnp.int32), axis=1) - 1

    def masked_scores(start):
        query_block = lax.dynamic_slice_in_dim(queries, start, block, 0)
        raw = jnp.einsum("qhd,khd->hqk", query_block, keys, preferred_element_type=jnp.float32)
        rows = start + jnp.arange(block, dtype=jnp.int32)
        row_seg = lax.dynamic_slice_in_dim(segment, start, block, 0)
        allowed = (positions[None, :] <= rows[:, None]) & (segment[None, :] == row_seg[:, None])
        return (query_block, jnp.where(allowed[None], raw, NEG))

    def forward_block(index):
        query_block, masked = masked_scores(index * block)
        top = jnp.max(masked, axis=-1, keepdims=True)
        expo = jnp.exp(masked - top)
        total = jnp.sum(expo, axis=-1, keepdims=True)
        probs = (expo / total).astype(jnp.bfloat16)
        attended = jnp.einsum("hqk,khd->qhd", probs, values, preferred_element_type=jnp.float32)
        return (attended.astype(jnp.bfloat16), (top + jnp.log(total))[..., 0])

    head_out, log_totals = lax.map(forward_block, jnp.arange(blocks, dtype=jnp.int32))
    head_out = head_out.reshape(length, local_width)
    attn_rows = lax.all_to_all(head_out, "seq", split_axis=0, concat_axis=1, tiled=True)
    mixed = resid + jnp.dot(attn_rows, w_out, preferred_element_type=jnp.float32)
    normed_two, inverse_two, hidden_two = norm_forward(mixed, gain_two)
    gate = jnp.dot(hidden_two, w_up, preferred_element_type=jnp.float32)
    sigma = jax.nn.sigmoid(gate)
    activ = (gate * sigma).astype(jnp.bfloat16)
    outputs = mixed + jnp.dot(activ, w_down, preferred_element_type=jnp.float32)
    grad_top = cotangent[0]
    grad_low = grad_top.astype(jnp.bfloat16)
    grad_activ = jnp.dot(grad_low, w_down.T, preferred_element_type=jnp.float32)
    grad_gate = (grad_activ * sigma * (1.0 + gate * (1.0 - sigma))).astype(jnp.bfloat16)
    grad_down = jnp.dot(activ.T, grad_low, preferred_element_type=jnp.float32)
    grad_up = jnp.dot(hidden_two.T, grad_gate, preferred_element_type=jnp.float32)
    grad_hidden_two = jnp.dot(grad_gate, w_up.T, preferred_element_type=jnp.float32)
    grad_norm_two, gain_grad_two = norm_backward(grad_hidden_two, normed_two, inverse_two, gain_two)
    grad_mixed = grad_top + grad_norm_two
    mixed_low = grad_mixed.astype(jnp.bfloat16)
    grad_out = jnp.dot(attn_rows.T, mixed_low, preferred_element_type=jnp.float32)
    grad_attn = jnp.dot(mixed_low, w_out.T, preferred_element_type=jnp.float32).astype(jnp.bfloat16)
    grad_heads = lax.all_to_all(grad_attn, "seq", split_axis=1, concat_axis=0, tiled=True).reshape(
        length, local_heads, head_dim
    )

    def backward_block(carry, index):
        key_sum, value_sum = carry
        start = index * block
        query_block, masked = masked_scores(start)
        grad_block = lax.dynamic_slice_in_dim(grad_heads, start, block, 0)
        lse_block = log_totals[index]
        probs = jnp.exp(masked - lse_block[:, :, None])
        value_sum = value_sum + jnp.einsum(
            "hqk,qhd->khd",
            probs.astype(jnp.bfloat16),
            grad_block,
            preferred_element_type=jnp.float32,
        )
        grad_probs = jnp.einsum(
            "qhd,khd->hqk", grad_block, values, preferred_element_type=jnp.float32
        )
        grad_scores = probs * (grad_probs - jnp.sum(probs * grad_probs, axis=-1, keepdims=True))
        scores_low = grad_scores.astype(jnp.bfloat16)
        grad_query = jnp.einsum(
            "hqk,khd->qhd", scores_low, keys, preferred_element_type=jnp.float32
        )
        key_sum = key_sum + jnp.einsum(
            "hqk,qhd->khd", scores_low, query_block, preferred_element_type=jnp.float32
        )
        return ((key_sum, value_sum), grad_query)

    empty = jnp.zeros((length, local_heads, head_dim), jnp.float32)
    (key_grad, value_grad), query_grad = lax.scan(
        backward_block, (empty, empty), jnp.arange(blocks, dtype=jnp.int32)
    )
    stacked = jnp.stack(
        [
            query_grad.reshape(length, local_width),
            key_grad.reshape(length, local_width),
            value_grad.reshape(length, local_width),
        ],
        axis=1,
    ).astype(jnp.bfloat16)
    returned = lax.all_to_all(stacked, "seq", split_axis=0, concat_axis=2, tiled=True)
    scaled_grad = returned[:, 0].astype(jnp.float32)
    scale_part = jnp.sum(scaled_grad * projected[:, 0], axis=0).reshape(HEADS, head_dim).sum(axis=0)
    query_low = (scaled_grad * tiled[None]).astype(jnp.bfloat16)
    grad_qkv_rows = jnp.concatenate([query_low[:, None], returned[:, 1:]], axis=1).reshape(
        count, 3 * width
    )
    grad_qkv = jnp.dot(hidden_one.T, grad_qkv_rows, preferred_element_type=jnp.float32)
    grad_hidden_one = jnp.dot(grad_qkv_rows, w_qkv.T, preferred_element_type=jnp.float32)
    grad_norm_one, gain_grad_one = norm_backward(grad_hidden_one, normed_one, inverse_one, gain_one)
    input_grad = grad_mixed + grad_norm_one
    all_grads = jnp.concatenate([grad_qkv, grad_out, grad_up, grad_down], axis=1)
    gain_grads = jnp.stack([gain_grad_one, gain_grad_two])
    owned_w, owned_g = (
        lax.psum_scatter(
            all_grads.astype(jnp.bfloat16), "dp", scatter_dimension=0, tiled=True
        ).astype(jnp.float32),
        lax.psum_scatter(
            gain_grads.astype(jnp.bfloat16), "dp", scatter_dimension=1, tiled=True
        ).astype(jnp.float32),
    )
    owned_w, owned_g = (
        lax.psum(owned_w.astype(jnp.bfloat16), "seq").astype(jnp.float32),
        lax.psum(owned_g.astype(jnp.bfloat16), "seq").astype(jnp.float32),
    )
    scale_grad = lax.psum(scale_part, ("dp", "seq")) * base_scale * jax.nn.sigmoid(qscale)
    weights_new, weight_m_new, weight_v_new = adamw(
        weights, owned_w, weight_m, weight_v, RATE_MATRIX
    )
    gains_new, gain_m_new, gain_v_new = adamw(gains, owned_g, gain_m, gain_v, RATE_GAIN)
    qscale_new, qscale_m_new, qscale_v_new = adamw(
        qscale, scale_grad, qscale_m, qscale_v, RATE_GAIN
    )
    return (
        outputs[None],
        input_grad[None],
        weights_new,
        weight_m_new,
        weight_v_new,
        weights_new.astype(jnp.bfloat16),
        gains_new,
        gain_m_new,
        gain_v_new,
        qscale_new,
        qscale_m_new,
        qscale_v_new,
    )


MESH = pl.DeviceIdType.MESH
BF = jnp.bfloat16
F32 = jnp.float32
DEPTH = 4
STEP_ROWS = 32
UNITS = 8
FIRST_X = ("d", "D")
VMEM_BYTES = 64 * 1024 * 1024


class Hop:
    def __init__(self, number, sems, source, target, arriving, device, when=None, into=None):
        self.number, self.when, self.pending = number, when, True
        self.out = self.describe(number, into or number, sems, source, target, device)
        if arriving is not None:
            self.back = self.describe(number, number, sems, arriving, arriving, device)
        self.guard(self.out.start)

    @staticmethod
    def describe(number, into, sems, source, target, device):
        return pltpu.make_async_remote_copy(
            src_ref=source,
            dst_ref=target,
            send_sem=sems[0].at[number],
            recv_sem=sems[1].at[into],
            device_id=device,
            device_id_type=MESH,
        )

    def guard(self, action):
        if self.when is None:
            action()
        else:
            pl.when(self.when)(action)

    def arrived(self):
        self.back.wait_recv()

    def left(self):
        if self.pending:
            self.guard(self.out.wait_send)
        self.pending = False


def dot_nn(left, right):
    return lax.dot_general(left, right, (((1,), (0,)), ((), ())), preferred_element_type=F32)


def dot_nt(left, right):
    return lax.dot_general(left, right, (((1,), (1,)), ((), ())), preferred_element_type=F32)


def dot_tn(left, right):
    return lax.dot_general(left, right, (((0,), (0,)), ((), ())), preferred_element_type=F32)


def inverse_rms(rows):
    return lax.rsqrt(jnp.mean(rows * rows, axis=-1, keepdims=True) + EPS)


def loop(count, body):
    def step(index, carry):
        body(index)
        return carry

    lax.fori_loop(0, count, step, 0)


def scratch_plan(count, width, half, rows):
    length = 2 * count
    blocks = (DEPTH, 2, 2, rows, half)
    return dict(
        x=((count, width), F32),
        x2=((count, width), F32),
        cd=((count, width), F32),
        dh=((count, width), F32),
        qf=((length, half), F32),
        h1=((length, width), BF),
        gb=((2, count, width), BF),
        du=((2, count, width), BF),
        ab=((2, count, half), BF),
        abh=((2, length, half), BF),
        of=((2, length, half), BF),
        dos=((count, half), BF),
        dof=((length, half), BF),
        qkv=((3, length, half), BF),
        dq=((2, 3, length, half), BF),
        tz=((2 * DEPTH, 2, rows, count), BF),
        th=((2 * DEPTH, 2, rows, count), BF),
        to=((2 * DEPTH, 2, rows, length), BF),
        tzr=((2 * DEPTH, rows, count), BF),
        thr=((2 * DEPTH, rows, count), BF),
        tor=((2 * DEPTH, rows, length), BF),
        t1=((2 * DEPTH, 2, rows, length), BF),
        t1r=((2 * DEPTH, rows, length), BF),
        bias=((3 * count, count), F32),
        p0=((8, count, count), BF),
        p1=((8, length, count), BF),
        dh1r=((count, width), BF),
        wst=((UNITS, rows, half), F32),
        w=((9,) + blocks, BF),
        s=((8, DEPTH, 2, rows, half), BF),
        yr=((DEPTH, 2, rows, half), BF),
        xr=((7, DEPTH, rows, half), BF),
        zr=((7, DEPTH - 1, rows, half), BF),
        g=((12, rows, half), BF),
        go=((2, rows, half), BF),
        gr=((2, rows, half), BF),
        gn=((DEPTH, 2, 2, rows, 128), BF),
        gs=((128, 128), F32),
        fs=((8, half), F32),
        gt=((8, width), F32),
        dg=((2, 8, width), F32),
        sm=((4, 8, width), F32),
        smr=((3, 8, width), F32),
        smz=((DEPTH, 8, width), F32),
    )


HOPS = 176
ORDER = (
    "gz", "stup", "stD", "stv", "stO", "std", "stk", "sto", "bias", "stq", "gx", "gb", "zav",
    "zaup", "gc", "h1", "zak", "ziv", "zaq", "ziup", "zbv", "zao", "zik", "zbup", "zaO", "szd",
    "ziq", "h1_", "t1", "zbk", "zio", "fxv", "zad", "szD", "ziO", "Pv", "zbq", "zbo", "fxup",
    "zid", "zaD", "zbO", "fxk", "Pk", "ziD", "fxq", "zbd", "Pq", "A0", "A1", "A2", "A3", "A4",
    "A5", "A6", "A7", "so", "fxo", "fyup", "fxO", "zbD", "x2", "h2", "u", "tz", "dz", "dh2", "dx2",
    "do0", "Wd", "do1", "to", "out", "axd01", "th", "axd02", "B0", "B1", "axd03", "B2", "B3",
    "axd00", "B4", "B5", "axd11", "B6", "B7", "azd0", "axd12", "dvk", "dq", "Wup", "axd13", "abc",
    "Wv", "Wk", "Wq", "dhp", "axv1", "Wo", "aed0", "axd10", "azd1", "axv2", "dho", "axv3", "axv0",
    "axk1", "azv", "axk2", "ayup", "axk3", "axk0", "axq1", "azk", "axq2", "axq3", "axq0", "ig",
    "axo1", "aed1", "smx", "azq", "axo2", "aev", "aek", "axo3", "aeq", "axo0", "axup1", "azo",
    "axup2", "axup3", "aeo", "axup0", "smy", "smz", "azup", "sme", "aeup",
)


def layer_kernel(
    names, head_dim, x_hbm, cot_hbm, starts, w_hbm, gains_own, qscale,
    out_hbm, grad_in_hbm, grad_hbm, small_hbm, *scratch
):
    m = types.SimpleNamespace(**dict(zip(names, scratch[: len(names)])))
    send_sems, recv_sems, load_sems, store_sems = scratch[len(names):]
    sems = (send_sems, recv_sems)
    count, width = m.x.shape
    length, half = m.dof.shape
    rows = m.wst.shape[1]
    heads = half // head_dim

    me = lax.axis_index("dp")
    y = lax.axis_index("seq")
    z = lax.div(me, 4)
    x = lax.rem(lax.div(me, 2), 2)
    c = lax.rem(me, 2)
    oy, ox, oc = 1 - y, 1 - x, 1 - c
    to_y = {"seq": oy}
    to_x = {"dp": 4 * z + 2 * ox + c}
    to_c = {"dp": 4 * z + 2 * x + oc}
    up_z = [lax.rem(z + k, DEPTH) for k in range(DEPTH)]
    down_z = [lax.rem(z + DEPTH - k, DEPTH) for k in range(DEPTH)]
    to_z = [{"dp": 4 * up_z[k] + 2 * x + c} for k in range(DEPTH)]
    inner = (z == 1) | (z == 2)
    near_z = z + 1 - 2 * lax.rem(z, 2)
    to_near = {"dp": 4 * near_z + 2 * x + c}
    to_middle = {"dp": 4 * (DEPTH - 1 - z) + 2 * x + c}
    outer = jnp.logical_not(inner)
    near_first = 2 * lax.div(z, 2)
    far_first = 2 - near_first
    near, far = pl.ds(near_first, 2), pl.ds(far_first, 2)
    hops = []

    def send(source, target, arriving, device, when=None, into=None):
        one = Hop(len(hops), sems, source, target, arriving, device, when, into)
        hops.append(one)
        return one

    own_row = pl.multiple_of(y * count, count)
    peer_row = pl.multiple_of(oy * count, count)

    names_of = ["v", "k", "q", "up", "o", "O", "d", "D"]
    unit_part = [2, 1, 0, 4, 3, 3, 5, 5]
    unit_half = [y, y, y, y, y, oy, y, oy]
    unit_slot = [2, 1, 0, 5 + y, 3 + y, 3 + oy, 7 + y, 7 + oy]
    swap_slot = 5 + oy
    loads = []
    for u in range(UNITS):
        start = pl.multiple_of(unit_part[u] * width + unit_half[u] * half, 128)
        loads.append(
            pltpu.make_async_copy(w_hbm.at[:, pl.ds(start, half)], m.wst.at[u], load_sems.at[u])
        )
        loads[u].start()
    load_x = pltpu.make_async_copy(x_hbm, m.x, load_sems.at[UNITS])
    load_cot = pltpu.make_async_copy(cot_hbm, m.cd, load_sems.at[UNITS + 1])
    load_x.start()
    load_cot.start()
    steps = {}

    def step(name):
        def keep(body):
            steps[name] = body
            return body

        return keep

    barrier = pltpu.get_barrier_semaphore()
    for device in (to_y, to_x, to_c, to_z[1], to_z[2], to_z[3]):
        pl.semaphore_signal(barrier, inc=1, device_id=device, device_id_type=MESH)
    m.gs[...] = jnp.zeros_like(m.gs)
    m.gs[0:2, 0:rows] = gains_own[...]
    m.gn[z, x, c] = jnp.transpose(m.gs[...])[:rows].astype(BF)
    stretch = jnp.maximum(qscale[...], 0.0) + jnp.log1p(jnp.exp(-jnp.abs(qscale[...])))
    m.fs[...] = jnp.zeros_like(m.fs)
    m.fs[0:1, 0:head_dim] = QUERY_BASE / math.sqrt(head_dim) * stretch
    one_head = m.fs[...]
    every = one_head
    for head in range(1, heads):
        every = every + pltpu.roll(one_head, head * head_dim, 1)
    m.fs[...] = every
    factor = m.fs.at[0:1]
    pl.semaphore_wait(barrier, 6)

    hop = {}

    @step("gz")
    def _():
        block = m.gn.at[z, x, c]
        for k in range(1, DEPTH):
            hop["gz", k] = send(block, block, m.gn.at[down_z[k], x, c], to_z[k])

    @step("gx")
    def _():
        for k in range(1, DEPTH):
            hop["gz", k].arrived()
        block = m.gn.at[:, x, c]
        hop["gx"] = send(block, block, m.gn.at[:, ox, c], to_x)

    @step("gc")
    def _():
        hop["gx"].arrived()
        block = m.gn.at[:, :, c]
        hop["gc"] = send(block, block, m.gn.at[:, :, oc], to_c)

    @step("gb")
    def _():
        load_cot.wait()

        def make_gb(index):
            at = pl.ds(index * STEP_ROWS, STEP_ROWS)
            m.gb[0, at] = m.cd[at].astype(BF)

        loop(count // STEP_ROWS, make_gb)
        hop["gb"] = send(m.gb.at[0], m.gb.at[1], m.gb.at[1], to_c)

    @step("bias")
    def _():
        def make_bias(first, offset):
            position = lax.broadcasted_iota(jnp.int32, (1, count), 1) + first
            begin = jnp.zeros((1, count), jnp.int32)
            for j in range(starts.shape[1]):
                begin = jnp.maximum(begin, jnp.where(starts[0, j] <= position, starts[0, j], 0))

            def fill(index):
                key = lax.broadcasted_iota(jnp.int32, (STEP_ROWS, count), 0) + index * STEP_ROWS
                kept = (key <= position) & (key >= begin)
                at = pl.ds(pl.multiple_of(offset + index * STEP_ROWS, STEP_ROWS), STEP_ROWS)
                m.bias[at] = jnp.where(kept, 0.0, NEG)

            loop((first + count) // STEP_ROWS, fill)

        make_bias(0, 0)
        make_bias(count, count)
        m.of[y] = jnp.zeros_like(m.of[y])
        m.dq[0] = jnp.zeros_like(m.dq[0])
        m.dg[...] = jnp.zeros_like(m.dg)

    h1_own, h1_peer = m.h1.at[pl.ds(own_row, count)], m.h1.at[pl.ds(peer_row, count)]

    @step("h1")
    def _():
        load_x.wait()
        hop["gc"].arrived()
        gains = m.gn[...].reshape(width, 128).astype(F32)
        m.gt[...] = jnp.transpose(gains)[:8]

        def make_h1(index):
            values = m.x[pl.ds(index * STEP_ROWS, STEP_ROWS)]
            normed = values * inverse_rms(values)
            at = pl.ds(pl.multiple_of(own_row + index * STEP_ROWS, STEP_ROWS), STEP_ROWS)
            m.h1[at] = (normed * m.gt[0:1]).astype(BF)

        loop(count // STEP_ROWS, make_h1)
        hop["h1"] = send(h1_own, h1_own, h1_peer, to_y)

    def unit_steps(u, first_x):
        name, slot = names_of[u], unit_slot[u]
        side = slice(None) if first_x else x

        def pair_start():
            block = m.w.at[slot, z, side, c]
            hop["za", u] = send(block, block, m.w.at[slot, near_z, side, c], to_near)

        @step("st" + name)
        def _():
            loads[u].wait()
            m.w[slot, z, x, c] = m.wst[u].astype(BF)
            if first_x:
                block = m.w.at[slot, z, x, c]
                hop["xo", u] = send(block, block, m.w.at[slot, z, ox, c], to_x)
            else:
                pair_start()

        @step("sz" + name)
        def _():
            hop["xo", u].arrived()
            pair_start()

        @step("za" + name)
        def _():
            hop["za", u].arrived()
            block = m.w.at[slot, near, side, c]
            hop["zb", u] = send(
                block, block, m.w.at[slot, far, side, c], to_middle, when=inner
            )
            if not first_x:
                hop["xa", u] = send(block, block, m.w.at[slot, near, ox, c], to_x)

        @step("zi" + name)
        def _():
            pl.when(inner)(hop["zb", u].arrived)
            block = m.w.at[slot, far, side, c]
            hop["zc", u] = send(
                block, block, None, to_near, when=inner, into=hop["zb", u].number
            )

        @step("zb" + name)
        def _():
            pl.when(outer)(hop["zb", u].arrived)
            if first_x:
                block = m.w.at[slot, :, :, c]
                hop["c", u, 1] = send(block, block, m.w.at[slot, :, :, oc], to_c)
                return
            block = m.w.at[slot, far, x, c]
            hop["xb", u] = send(block, block, m.w.at[slot, far, ox, c], to_x)
            block = m.w.at[slot, :, x, c]
            hop["c", u, 0] = send(block, block, m.w.at[slot, :, x, oc], to_c)

        @step("fx" + name)
        def _():
            hop["xa", u].arrived()
            hop["xb", u].arrived()
            if name == "up":
                block = m.w.at[slot, :, :, c]
                hop["y", u] = send(block, block, m.w.at[swap_slot, :, :, c], to_y)
            block = m.w.at[slot, :, ox, c]
            hop["c", u, 1] = send(block, block, m.w.at[slot, :, ox, oc], to_c)

        @step("fy" + name)
        def _():
            hop["y", u].arrived()
            block = m.w.at[swap_slot, :, :, c]
            hop["yc", u] = send(block, block, m.w.at[swap_slot, :, :, oc], to_c)

    for u in range(UNITS):
        unit_steps(u, names_of[u] in FIRST_X)

    def ready(*wanted):
        for name in wanted:
            u = names_of.index(name)
            if ("c", u, 0) in hop:
                hop["c", u, 0].arrived()
            hop["c", u, 1].arrived()
            if name == "up":
                hop["yc", u].arrived()

    def weight(slot):
        return m.w[slot].reshape(width, half)

    def project(part):
        def block(index):
            at = pl.ds(pl.multiple_of(index * count, count), count)
            result = dot_nn(m.h1[at], weight(part))
            if part == 0:
                m.qf[at] = result
                result = result * factor[...]
            m.qkv[part, at] = result.astype(BF)

        loop(2, block)

    @step("t1")
    def _():
        def transpose_h1(index):
            at = pl.ds(pl.multiple_of(index * count, count), count)
            m.t1[:, :, :, at] = jnp.transpose(m.h1[at]).reshape(2 * DEPTH, 2, rows, count)

        loop(2, transpose_h1)
        hop["t1"] = send(m.t1.at[:, oc], m.t1r, m.t1r, to_c)

    def project_step(name):
        def body():
            ready(name)
            project("qkv".index(name))

        return body

    for name in "qkv":
        steps["P" + name] = project_step(name)

    def head_window(head):
        first = min(head * head_dim // 128 * 128, half - 256)
        lane = lax.broadcasted_iota(jnp.int32, (1, 256), 1) + first
        inside = (lane >= head * head_dim) & (lane < (head + 1) * head_dim)
        return slice(first, first + 256), jnp.where(inside, 1.0, 0.0).astype(BF)

    def attend(head):
        window, mask = head_window(head)
        keys = m.qkv[1, :, window]
        queries = m.qkv[0, :, window] * mask
        values = m.qkv[2, :, window] * mask
        for b in range(2):
            at, upto = slice(b * count, (b + 1) * count), (b + 1) * count
            allowed = m.bias[pl.ds(b * count, upto)]
            scores = dot_nt(keys[:upto], queries[at]) + allowed
            top = jnp.max(scores, axis=0, keepdims=True)
            expo = jnp.exp(scores - top)
            total = jnp.sum(expo, axis=0, keepdims=True)
            probs = (expo * (1.0 / total)).astype(BF)
            kept = m.p1 if b else m.p0
            kept[head] = probs
            found = dot_tn(probs, values[:upto])
            m.of[y, at, window] = m.of[y, at, window] + found.astype(BF)

    for head in range(heads):
        steps[f"A{head}"] = functools.partial(attend, head)

    own_rows, peer_rows = pl.ds(own_row, count), pl.ds(peer_row, count)

    @step("so")
    def _():
        block = m.of.at[y, peer_rows]
        hop["o"] = send(block, block, m.of.at[oy, own_rows], to_y)
        block = m.of.at[y, own_rows]
        hop["o2"] = send(block, block, m.of.at[oy, peer_rows], to_y)

    @step("to")
    def _():
        hop["o2"].arrived()

        def transpose_o(index):
            m.to[pl.ds(index * DEPTH, DEPTH)] = jnp.transpose(m.of[index]).reshape(
                DEPTH, 2, rows, length
            )

        loop(2, transpose_o)
        hop["to"] = send(m.to.at[:, oc], m.tor, m.tor, to_c)

    def mix(index):
        at = pl.ds(pl.multiple_of(index * half, 128), half)
        right = weight(3 + index)
        m.x2[:, at] = m.x[:, at] + (
            dot_nn(m.of[0, own_rows], right[:half]) + dot_nn(m.of[1, own_rows], right[half:])
        )

    @step("x2")
    def _():
        hop["o"].arrived()
        ready("o", "O")
        loop(2, mix)

    def make_h2(index):
        at = pl.ds(pl.multiple_of(index * STEP_ROWS, STEP_ROWS), STEP_ROWS)
        values = m.x2[at]
        normed = values * inverse_rms(values)
        m.h1[at] = (normed * m.gt[1:2]).astype(BF)

    h2, act = m.h1.at[pl.ds(0, count)], m.h1.at[pl.ds(count, count)]

    @step("h2")
    def _():
        hop["h1"].left()
        loop(count // STEP_ROWS, make_h2)

    @step("th")
    def _():
        m.th[...] = jnp.transpose(h2[...]).reshape(2 * DEPTH, 2, rows, count)
        hop["th"] = send(m.th.at[:, oc], m.thr, m.thr, to_c)

    def back(left, slot, index):
        at = pl.ds(2 * index, 2)
        return dot_nt(left[0], m.w[slot, at].reshape(half, half)) + dot_nt(
            left[1], m.w[slot + 1, at].reshape(half, half)
        )

    def halves(whole_rows):
        return whole_rows[:, :half], whole_rows[:, half:]

    def feed(index):
        at = pl.ds(pl.multiple_of(index * half, 128), half)
        gate = dot_nn(h2[...], weight(5 + index))
        m.dh[:, at] = gate
        act[:, at] = (gate / (1.0 + jnp.exp(-gate))).astype(BF)

    @step("u")
    def _():
        ready("up")
        loop(2, feed)

    @step("tz")
    def _():
        m.tz[...] = jnp.transpose(act[...]).reshape(2 * DEPTH, 2, rows, count)
        hop["tz"] = send(m.tz.at[:, oc], m.tzr, m.tzr, to_c)

    def gate_back(index):
        at = pl.ds(pl.multiple_of(index * half, 128), half)
        gate = m.dh[:, at]
        sigma = 1.0 / (1.0 + jnp.exp(-gate))
        grad = back(halves(m.gb[0]), 7, index)
        m.du[0, :, at] = (grad * sigma * (1.0 + gate * (1.0 - sigma))).astype(BF)

    @step("dz")
    def _():
        ready("d", "D")
        loop(2, gate_back)
        hop["du"] = send(m.du.at[0], m.du.at[1], m.du.at[1], to_c)

    def weight_grad(slot, here, there, rights):
        def block(index):
            right_here, right_there = rights()
            at = pl.ds(DEPTH * index, DEPTH)
            depth = here.shape[-1]
            total = dot_nn(here[at, c].reshape(DEPTH * rows, depth), right_here)
            total = total + dot_nn(there[at].reshape(DEPTH * rows, depth), right_there)
            m.s[slot, pl.ds(2 * index, 2)] = total.astype(BF).reshape(2, 2, rows, half)

        loop(2, block)

    def column_grad(first, here, there, right):
        def one(index):
            at = pl.ds(pl.multiple_of(index * half, 128), half)
            weight_grad(first + index, here, there, lambda: (right[0, :, at], right[1, :, at]))

        loop(2, one)

    sum_names = ["q", "k", "v", "o", "up", "d0", "d1"]
    sum_slot = [0, 1, 2, 3, 4 + y, 6, 7]
    whole = {5: 0, 6: 1}
    columns = [0, 2, 4, 6, 8, 10, 11]

    def start_x(name):
        u = sum_names.index(name)
        for k in (1, 2, 3, 0):
            target = m.xr.at[u, up_z[k]]
            hop["sx", u, k] = send(m.s.at[sum_slot[u], up_z[k], ox], target, target, to_x)

    @step("ayup")
    def _():
        hop["sy"].arrived()
        slot = sum_slot[4]

        def block(index):
            for k in range(2):
                total = m.s[slot, index, k].astype(F32) + m.yr[index, k].astype(F32)
                m.s[slot, index, k] = total.astype(BF)

        loop(DEPTH, block)
        start_x("up")

    def sum_steps(u):
        name, slot = sum_names[u], sum_slot[u]

        def add_x(k):
            def body():
                hop["sx", u, k].arrived()
                target = up_z[k]
                total = m.s[slot, target, x].astype(F32) + m.xr[u, target].astype(F32)
                m.s[slot, target, x] = total.astype(BF)
                if k:
                    there = m.zr.at[u, k - 1]
                    hop["sz", u, k] = send(m.s.at[slot, target, x], there, there, to_z[k])

            return body

        for k in range(DEPTH):
            steps[f"ax{name}{k}"] = add_x(k)

        @step("az" + name)
        def _():
            total = m.s[slot, z, x].astype(F32)
            for k in range(1, DEPTH):
                hop["sz", u, k].arrived()
                total = total + m.zr[u, k - 1].astype(F32)
            if u in whole:
                mine, other = m.go.at[whole[u]], m.gr.at[whole[u]]
                mine[...] = total.astype(BF)
                hop["se", u] = send(mine, other, other, to_y)
            else:
                mine, other = m.g.at[columns[u] + y], m.g.at[columns[u] + oy]
                mine[...] = total.astype(BF)
                hop["se", u] = send(mine, mine, other, to_y)

        @step("ae" + name)
        def _():
            hop["se", u].arrived()
            ready_columns = [columns[u]]
            if u in whole:
                total = m.go[whole[u]].astype(F32) + m.gr[whole[u]].astype(F32)
                m.g[columns[u]] = total.astype(BF)
            else:
                ready_columns.append(columns[u] + 1)
            for column in ready_columns:
                store(m.g.at[column], grad_hbm.at[:, pl.ds(column * half, half)])

    for u in range(len(sum_names)):
        sum_steps(u)

    stores = []

    def store(source, target):
        copy = pltpu.make_async_copy(source, target, store_sems.at[len(stores)])
        copy.start()
        stores.append(copy)

    @step("Wd")
    def _():
        hop["tz"].arrived()
        hop["gb"].arrived()
        column_grad(6, m.tz, m.tzr, m.gb)
        start_x("d0")
        start_x("d1")

    @step("Wup")
    def _():
        hop["th"].arrived()
        hop["du"].arrived()
        column_grad(4, m.th, m.thr, m.du)
        hop["sy"] = send(m.s.at[4 + oy], m.yr, m.yr, to_y)

    @step("Wo")
    def _():
        hop["to"].arrived()
        hop["abc"].arrived()
        weight_grad(3, m.to, m.tor, lambda: (m.abh[0], m.abh[1]))
        start_x("o")

    def feed_back(index):
        at = pl.ds(pl.multiple_of(index * half, 128), half)
        m.dh[:, at] = back(halves(m.du[0]), 5, index)

    @step("dh2")
    def _():
        loop(2, feed_back)

    def norm_back(values, inverse, gain, grad):
        normed = values * inverse
        scaled = grad * gain
        mean = jnp.mean(scaled * normed, axis=-1, keepdims=True)
        part = jnp.sum((grad * normed).reshape(STEP_ROWS // 8, 8, width), axis=0)
        return inverse * (scaled - normed * mean), part

    def make_dx2(index):
        at = pl.ds(pl.multiple_of(index * STEP_ROWS, STEP_ROWS), STEP_ROWS)
        values = m.x2[at]
        grad, part = norm_back(values, inverse_rms(values), m.gt[1:2], m.dh[at])
        m.dg[1] = m.dg[1] + part
        total = m.cd[at] + grad
        m.cd[at] = total
        m.ab[0, at], m.ab[1, at] = halves(total.astype(BF))

    @step("dx2")
    def _():
        loop(count // STEP_ROWS, make_dx2)

    @step("do0")
    def _():
        m.dos[...] = back((m.ab[0], m.ab[1]), 3, oy).astype(BF)
        target, arriving = m.dof.at[pl.ds(own_row, count)], m.dof.at[pl.ds(peer_row, count)]
        hop["do"] = send(m.dos, target, arriving, to_y)
        m.abh[0, own_rows] = m.ab[y]
        target, arriving = m.abh.at[0, own_rows], m.abh.at[0, peer_rows]
        hop["ab"] = send(m.ab.at[oy], target, arriving, to_y)

    @step("abc")
    def _():
        hop["ab"].arrived()
        hop["abc"] = send(m.abh.at[0], m.abh.at[1], m.abh.at[1], to_c)

    @step("do1")
    def _():
        m.dof[pl.ds(own_row, count)] = back((m.ab[0], m.ab[1]), 3, y).astype(BF)

    def finish_out(index):
        at = pl.ds(pl.multiple_of(index * half, 128), half)
        m.x2[:, at] = m.x2[:, at] + dot_nn(act[...], weight(7 + index))

    @step("out")
    def _():
        loop(2, finish_out)
        store(m.x2, out_hbm)

    def attend_back(head):
        window, mask = head_window(head)
        masked_keys = m.qkv[1, :, window] * mask
        queries = m.qkv[0, :, window] * mask
        values = m.qkv[2, :, window]
        grads = m.dof[:, window] * mask
        key_sum, value_sum = None, None
        for b in (1, 0):
            at, upto = slice(b * count, (b + 1) * count), (b + 1) * count
            low_probs = m.p1[head] if b else m.p0[head]
            probs = low_probs.astype(F32)
            grad_probs = dot_nt(values[:upto], grads[at])
            inner = jnp.sum(probs * grad_probs, axis=0, keepdims=True)
            low = (probs * (grad_probs - inner)).astype(BF)
            grad_query = dot_tn(low, masked_keys[:upto])
            m.dq[0, 0, at, window] = m.dq[0, 0, at, window] + grad_query.astype(BF)
            value_part = dot_nn(low_probs, grads[at])
            key_part = dot_nn(low, queries[at])
            if b:
                key_sum, value_sum = key_part[:count], value_part[:count]
                later = slice(count, length)
                m.dq[0, 1, later, window] = m.dq[0, 1, later, window] + key_part[count:].astype(BF)
                m.dq[0, 2, later, window] = m.dq[0, 2, later, window] + value_part[count:].astype(BF)
            else:
                m.dq[0, 1, at, window] = m.dq[0, 1, at, window] + (key_sum + key_part).astype(BF)
                m.dq[0, 2, at, window] = m.dq[0, 2, at, window] + (value_sum + value_part).astype(BF)

    def attend_back_step(head):
        def body():
            if head == 0:
                hop["do"].arrived()
            attend_back(head)

        return body

    for head in range(heads):
        steps[f"B{head}"] = attend_back_step(head)

    def share(part):
        hop["d", part] = send(m.dq.at[0, part], m.dq.at[1, part], m.dq.at[1, part], to_c)

    @step("dvk")
    def _():
        share(2)
        share(1)

    def scale_query(index):
        at = pl.ds(pl.multiple_of(index * STEP_ROWS, STEP_ROWS), STEP_ROWS)
        values = m.dq[0, 0, at].astype(F32)
        part = (values * m.qf[at]).reshape(STEP_ROWS // 8, 8, half)
        m.dg[0, :, :half] = m.dg[0, :, :half] + jnp.sum(part, axis=0)
        m.dq[0, 0, at] = (values * factor[...]).astype(BF)

    @step("dq")
    def _():
        loop(length // STEP_ROWS, scale_query)
        share(0)
        m.sm[0] = jnp.zeros_like(m.sm[0])
        m.sm[0, 2:3] = jnp.sum(m.dg[0], axis=0, keepdims=True)
        m.dg[0] = jnp.zeros_like(m.dg[0])

    def attention_weight(name):
        part = "qkv".index(name)

        def body():
            if name == "v":
                hop["t1"].arrived()
            hop["d", part].arrived()
            weight_grad(part, m.t1, m.t1r, lambda: (m.dq[0, part], m.dq[1, part]))
            start_x(name)

        return body

    for name in "qkv":
        steps["W" + name] = attention_weight(name)

    def hidden_back(row, index):
        at = pl.ds(2 * index, 2)
        total = None
        for part in range(3):
            term = dot_nt(
                m.dq[0, part, pl.ds(row, count)], m.w[part, at].reshape(half, half)
            )
            total = term if total is None else total + term
        return total

    def hidden_peer(index):
        at = pl.ds(pl.multiple_of(index * half, 128), half)
        h2[:, at] = hidden_back(peer_row, index).astype(BF)

    def hidden_own(index):
        at = pl.ds(pl.multiple_of(index * half, 128), half)
        m.dh[:, at] = hidden_back(own_row, index)

    @step("dhp")
    def _():
        loop(2, hidden_peer)
        hop["dh"] = send(h2, m.dh1r, m.dh1r, to_y)

    @step("dho")
    def _():
        loop(2, hidden_own)

    def make_input_grad(index):
        at = pl.ds(pl.multiple_of(index * STEP_ROWS, STEP_ROWS), STEP_ROWS)
        values = m.x[at]
        grad = m.dh[at] + m.dh1r[at].astype(F32)
        grad, part = norm_back(values, inverse_rms(values), m.gt[0:1], grad)
        m.dg[0] = m.dg[0] + part
        m.cd[at] = m.cd[at] + grad

    @step("ig")
    def _():
        hop["dh"].arrived()
        loop(count // STEP_ROWS, make_input_grad)
        store(m.cd, grad_in_hbm)
        for g in range(2):
            m.sm[0, g:g + 1] = jnp.sum(m.dg[g], axis=0, keepdims=True)
        hop["smc"] = send(m.sm.at[0], m.smr.at[0], m.smr.at[0], to_c)

    @step("smx")
    def _():
        hop["smc"].arrived()
        m.sm[1] = m.sm[0] + m.smr[0]
        hop["smx"] = send(m.sm.at[1], m.smr.at[1], m.smr.at[1], to_x)

    @step("smy")
    def _():
        hop["smx"].arrived()
        m.sm[2] = m.sm[1] + m.smr[1]
        hop["smy"] = send(m.sm.at[2], m.smr.at[2], m.smr.at[2], to_y)

    @step("smz")
    def _():
        hop["smy"].arrived()
        m.smz[z] = m.sm[2] + m.smr[2]
        block = m.smz.at[z]
        for k in range(1, DEPTH):
            hop["smz", k] = send(block, block, m.smz.at[down_z[k]], to_z[k])

    @step("sme")
    def _():
        for k in range(1, DEPTH):
            hop["smz", k].arrived()
        total = ((m.smz[0] + m.smz[1]) + m.smz[2]) + m.smz[3]
        m.sm[3] = total
        m.gs[0:8] = pltpu.roll(total, lax.rem(width - me * rows, width), 1)[:, :128]
        folded = m.sm[3, 2:3, 0:half]
        part = folded
        for head in range(1, heads):
            part = part + pltpu.roll(folded, half - head * head_dim, 1)
        m.gs[2:3] = part[:, :128]
        store(m.gs.at[0:8], small_hbm)

    for name in ORDER:
        if name == "h1_":
            hop["h1"].arrived()
        else:
            steps[name]()
    for one in hops:
        one.left()
    for copy in stores:
        copy.wait()


def fits(count, groups, owners, width, head_dim, rows):
    half = width // groups
    return (
        groups == 2
        and owners == 4 * DEPTH
        and count % 128 == 0
        and count % STEP_ROWS == 0
        and rows % 16 == 0
        and rows == width // owners
        and half % 128 == 0
        and half >= 256
        and half % head_dim == 0
        and (half // head_dim) % 4 == 0
        and head_dim <= 128
    )


def fused_layer(
    inputs,
    cotangent,
    starts,
    weights,
    weight_m,
    weight_v,
    gains,
    gain_m,
    gain_v,
    qscale,
    qscale_m,
    qscale_v,
):
    count, width = inputs.shape[1:]
    head_dim = width // HEADS
    groups = lax.axis_size("seq")
    half = width // groups
    rows, columns = weights.shape
    plan = scratch_plan(count, width, half, rows)
    anywhere = pl.BlockSpec(memory_space=pl.ANY)
    inside = pl.BlockSpec(memory_space=pltpu.VMEM)
    outputs, input_grad, grads, small = pl.pallas_call(
        functools.partial(layer_kernel, tuple(plan), head_dim),
        out_shape=(
            jax.ShapeDtypeStruct((count, width), F32),
            jax.ShapeDtypeStruct((count, width), F32),
            jax.ShapeDtypeStruct((rows, columns), BF),
            jax.ShapeDtypeStruct((8, 128), F32),
        ),
        in_specs=[
            anywhere,
            anywhere,
            pl.BlockSpec(memory_space=pltpu.SMEM),
            anywhere,
            inside,
            inside,
        ],
        out_specs=(anywhere,) * 4,
        scratch_shapes=[pltpu.VMEM(shape, kind) for shape, kind in plan.values()]
        + [
            pltpu.SemaphoreType.DMA((HOPS,)),
            pltpu.SemaphoreType.DMA((HOPS,)),
            pltpu.SemaphoreType.DMA((UNITS + 2,)),
            pltpu.SemaphoreType.DMA((15,)),
        ],
        compiler_params=pltpu.CompilerParams(
            collective_id=0, has_side_effects=True, vmem_limit_bytes=VMEM_BYTES
        ),
    )(inputs[0], cotangent[0], starts, weights, gains, qscale[None])
    steps = 5
    block = pl.BlockSpec((rows, columns // steps), lambda index: (0, index))
    pair = pl.BlockSpec((2, rows), lambda index: (0, 0))
    single = pl.BlockSpec((1, head_dim), lambda index: (0, 0))
    tokens = pl.BlockSpec((count, width // steps), lambda index: (0, index))
    matrix = jax.ShapeDtypeStruct((rows, columns), F32)
    result = pl.pallas_call(
        update_kernel,
        grid=(steps,),
        out_shape=(outputs, input_grad, matrix, matrix, matrix)
        + (jax.ShapeDtypeStruct((rows, columns), BF),)
        + (gains,) * 3
        + (jax.ShapeDtypeStruct((1, head_dim), F32),) * 3,
        in_specs=[tokens, tokens, block, pl.BlockSpec((8, 128), lambda index: (0, 0))]
        + [block] * 3
        + [pair] * 3
        + [single] * 3,
        out_specs=(tokens, tokens) + (block,) * 4 + (pair,) * 3 + (single,) * 3,
        compiler_params=pltpu.CompilerParams(vmem_limit_bytes=VMEM_BYTES),
    )(
        outputs, input_grad, grads, small, weights, weight_m, weight_v, gains, gain_m, gain_v,
        qscale[None], qscale_m[None], qscale_v[None],
    )
    return (result[0][None], result[1][None]) + tuple(result[2:9]) + tuple(
        value[0] for value in result[9:]
    )


def update_kernel(
    outputs, input_grad, grads, small, weights, weight_m, weight_v, gains, gain_m, gain_v,
    qscale, qscale_m, qscale_v, outputs_new, input_grad_new, weights_new, weight_m_new,
    weight_v_new, weights_low, gains_new, gain_m_new, gain_v_new, qscale_new, qscale_m_new,
    qscale_v_new
):
    outputs_new[...] = outputs[...]
    input_grad_new[...] = input_grad[...]
    head_dim = qscale.shape[1]

    @pl.when(pl.program_id(0) == 0)
    def _():
        gains_new[...], gain_m_new[...], gain_v_new[...] = adamw(
            gains[...], small[0:2, : gains.shape[1]], gain_m[...], gain_v[...], RATE_GAIN
        )
        slope = QUERY_BASE / math.sqrt(head_dim) / (1.0 + jnp.exp(-qscale[...]))
        qscale_new[...], qscale_m_new[...], qscale_v_new[...] = adamw(
            qscale[...], small[2:3, :head_dim] * slope, qscale_m[...], qscale_v[...], RATE_GAIN
        )

    updated, weight_m_new[...], weight_v_new[...] = adamw(
        weights[...], grads[...].astype(F32), weight_m[...], weight_v[...], RATE_MATRIX
    )
    weights_new[...] = updated
    weights_low[...] = updated.astype(BF)


def on_device(*arrays):
    count, width = arrays[0].shape[1:]
    rows = arrays[3].shape[0]
    if fits(count, lax.axis_size("seq"), lax.axis_size("dp"), width, width // HEADS, rows):
        return fused_layer(*arrays)
    return plain_layer(*arrays)


def solution(mesh):
    placed = (
        P("dp", "seq", None),
        P("dp", "seq", None),
        P("dp", None),
        P("dp", None),
        P("dp", None),
        P("dp", None),
        P(None, "dp"),
        P(None, "dp"),
        P(None, "dp"),
        P(),
        P(),
        P(),
    )
    return jax.shard_map(
        on_device,
        mesh=mesh,
        in_specs=placed,
        out_specs=placed[:2] + placed[3:6] + placed[5:],
        check_vma=False,
    )
```
